32 devices in a mesh: pipe: 4 (over y, x), dp: 8 (over z, core).
Axes of the slice: x: 2, y: 2, z: 4, core: 2. Of those that a mesh axis runs over, the one named last changes fastest.
Arguments:
- x_in: bfloat16 [4, 256, 4096], P(None, 'dp'), may hold values from -6 to 6
- cotangent: bfloat16 [4, 256, 4096], P(None, 'dp'), may hold values from -6 to 6
- weights: bfloat16 [4, 64, 64, 2048], P('pipe', 'dp'), as said below
- live_rows: int32 [4, 64, 32], P('pipe'), may hold values from 0 to 63, as said below
- moment: float32 [4, 64, 64, 2048], P('pipe', 'dp'), may hold values from -0.25 to 0.25
- second: float32 [4, 64, 64, 2048], P('pipe', 'dp'), may hold values from 4.8828126e-05 to 0.0009765625
Outputs:
- weights_out: bfloat16 [4, 64, 64, 2048], P('pipe', 'dp')
- moment_out: float32 [4, 64, 64, 2048], P('pipe', 'dp')
- second_out: float32 [4, 64, 64, 2048], P('pipe', 'dp')
The draws below stay inside these ranges and needn't reach their ends.
Inputs may be any that keep to these rules, and one draw needn't show every extreme that they name: `live_rows`: for each layer and block column the 32 entries are distinct block rows. `weights`: entry [l, j, b, k * 64 + a] is the weight from input feature live_rows[l, j, k] * 64 + a to output feature j * 64 + b; unstored blocks are zero.
All inputs are finite; a program needn't handle non-finite values.
Results may differ from the reference program's by a relative error of at most 0.009.
Values may be sent and summed in bfloat16 or wider, within the bound.
No kernel may reach another device: no remote copies, remote signals or barrier semaphores. Data moves between devices by JAX's collectives and lax.ppermute only.
A program may use at most 256 MiB of HBM per device.

```python
import math
import jax
import jax.numpy as jnp
from jax import lax

D = 4096
HEAD = 128
BLOCK = 64
MICRO = 4
TOK_DEV = 32
NB = 64
LIVE = 32
HEADS = 32
ROWS = 256
TOKENS = 1024
LAYERS = 4
N_DP = 8


def live_pattern(key):
    sub_key = jax.random.fold_in(key, 7)
    key_list = jax.random.split(sub_key, LAYERS * NB)
    shuffled = jax.vmap(lambda one_key: jax.random.permutation(one_key, NB))(key_list)
    return shuffled[:, :LIVE].reshape(LAYERS, NB, LIVE).astype(jnp.int32)


def draw_live_rows(key, part):
    return live_pattern(key)


def draw_weights(key, part):
    live_index = live_pattern(key)
    entry_key, head_key, block_key, column_key = jax.random.split(jax.random.fold_in(key, 11), 4)
    shape_five = (LAYERS, NB, BLOCK, LIVE, BLOCK)
    entries = jax.random.normal(entry_key, shape_five, jnp.float32)
    head_scale = jnp.exp(jax.random.uniform(head_key, (LAYERS, HEADS), jnp.float32, math.log(0.3), math.log(3.0)))
    block_scale = jnp.exp(jax.random.uniform(block_key, (LAYERS, NB, LIVE), jnp.float32, math.log(0.25), math.log(4.0)))
    column_scale = (1.0 + 2.0 * jnp.arange(NB, dtype=jnp.float32) / (NB - 1)) * jnp.exp(jax.random.uniform(column_key, (LAYERS, NB), jnp.float32, math.log(0.7), math.log(1.4)))
    layer_index = jnp.arange(LAYERS, dtype=jnp.int32)[:, None, None]
    row_scale = head_scale[layer_index, live_index // (HEAD // BLOCK)]
    factor = 0.3 / math.sqrt(LIVE * BLOCK) * row_scale * column_scale[:, :, None] * block_scale
    values = entries * factor[:, :, None, :, None]
    return values.reshape(LAYERS, NB, BLOCK, LIVE * BLOCK).astype(jnp.bfloat16)


def block_levels(rng, shape, shards, least, high):
    factor_of = 1.0
    for axis_at, parts in shards:
        draws = jax.random.uniform(jax.random.fold_in(jax.random.fold_in(rng, 6), axis_at), (parts,), jnp.float32, least / len(shards), high / len(shards))
        factor_of = factor_of * jnp.repeat(jnp.exp(draws), shape[axis_at] // parts).reshape((-1,) + (1,) * (len(shape) - 1 - axis_at))
    return factor_of


def normal_values(key, dims, deviation, bound, shards=(), kind=jnp.bfloat16):
    values = deviation * jax.random.normal(key, dims, jnp.float32)
    if shards:
        values = values * block_levels(key, dims, shards, -0.22, 0.18)
    return jnp.clip(values, -bound, bound).astype(kind)


def setup_inputs(seed: int = 0) -> dict:
    arg_keys = jax.random.split(jax.random.key(seed), 7)
    return {
        "x_in": normal_values(arg_keys[0], (MICRO, ROWS, D), 1.0, 6.0, ((1, 8),)),
        "cotangent": normal_values(arg_keys[1], (MICRO, ROWS, D), 1.0, 6.0, ((1, 8),)),
        "weights": draw_weights(jax.random.fold_in(arg_keys[6], 71), 0),
        "live_rows": draw_live_rows(jax.random.fold_in(arg_keys[6], 71), 0),
        "moment": normal_values(arg_keys[4], (LAYERS, NB, BLOCK, LIVE * BLOCK), (0.5 / TOKENS ** 0.5), 0.25, ((0, 4), (1, 8)), jnp.float32),
        "second": jnp.clip(jnp.exp(math.log(0.0009765625) - 2.9957323 * jax.random.uniform(arg_keys[5], (LAYERS, NB, BLOCK, LIVE * BLOCK), jnp.float32) ** block_levels(arg_keys[5], (LAYERS, NB, BLOCK, LIVE * BLOCK), ((0, 4), (1, 8)), -0.2, 0.2)), 4.882812572759576e-05, 0.0009765625),
    }


highest = lax.Precision.HIGHEST

def expand(packed, live_index):
    column_count, block_size, wide = packed.shape
    live_count = live_index.shape[1]
    values = packed.astype(jnp.float32).reshape(column_count, block_size, live_count, block_size).transpose(0, 2, 3, 1)
    column_ids = jnp.broadcast_to(jnp.arange(column_count, dtype=jnp.int32)[:, None], (column_count, live_count))
    expanded = jnp.zeros((column_count, block_size, column_count, block_size), jnp.float32)
    expanded = expanded.at[live_index, :, column_ids, :].set(values)
    return expanded.reshape(column_count * block_size, column_count * block_size)

def pack(expanded, live_index):
    column_count, live_count = live_index.shape
    column_ids = jnp.broadcast_to(jnp.arange(column_count, dtype=jnp.int32)[:, None], (column_count, live_count))
    four_way = expanded.reshape(column_count, BLOCK, column_count, BLOCK)[live_index, :, column_ids, :]
    return four_way.transpose(0, 3, 1, 2).reshape(column_count, BLOCK, live_count * BLOCK)

def weight_grad(normed, grad_pre, live_index):
    summed = jnp.zeros((NB, BLOCK, LIVE * BLOCK), jnp.float32)
    for member in range(N_DP):
        normed_part = normed[:, member * TOK_DEV:(member + 1) * TOK_DEV].reshape(-1, D).astype(jnp.float32)
        grad_part = grad_pre[:, member * TOK_DEV:(member + 1) * TOK_DEV].reshape(-1, D).astype(jnp.float32)
        expanded = jnp.dot(normed_part.T, grad_part, precision=highest) * (1.0 / TOKENS)
        rounded = lax.optimization_barrier(pack(expanded, live_index).astype(jnp.bfloat16))
        summed = summed + rounded.astype(jnp.float32)
    return summed

def shrink(magnitude, threshold):
    return jnp.maximum(magnitude - threshold, 0.0) / jnp.maximum(magnitude, threshold)

def tree_prox(stepped, live_index):
    blocked = stepped.reshape(NB, BLOCK, LIVE, BLOCK)
    magnitude = jnp.sqrt(lax.optimization_barrier(jnp.sum(blocked * blocked, axis=(1, 3))))
    leafed = blocked * shrink(magnitude, 0.15 * math.sqrt(BLOCK / LIVE))[:, None, :, None]
    block_squares = lax.optimization_barrier(jnp.sum(leafed * leafed, axis=(1, 3)))
    head_index = live_index // (HEAD // BLOCK)
    onehot = (head_index[:, :, None] == jnp.arange(HEADS, dtype=jnp.int32)[None, None, :]).astype(jnp.float32)
    head_squares = lax.optimization_barrier(jnp.sum(onehot * block_squares[:, :, None], axis=(0, 1)))
    head_factor = shrink(jnp.sqrt(head_squares), 0.45 * math.sqrt(HEAD))
    headed = leafed * lax.optimization_barrier(jnp.sum(onehot * head_factor[None, None, :], axis=2))[:, None, :, None]
    layer_squares = jnp.sum(headed * headed)
    layer_factor = shrink(jnp.sqrt(layer_squares), 0.45 * math.sqrt(D))
    return (headed * layer_factor).astype(jnp.bfloat16).reshape(NB, BLOCK, LIVE * BLOCK)

def reference(x_in, cotangent, weights, live_rows, moment, second):
    expanded_list = [expand(weights[layer], live_rows[layer]) for layer in range(LAYERS)]
    hidden = x_in
    saved = []
    for layer in range(LAYERS):
        as_float = hidden.astype(jnp.float32)
        inverse_rms = lax.rsqrt(lax.optimization_barrier(jnp.mean(as_float * as_float, axis=-1, keepdims=True)) + 1e-05)
        normed = (as_float * inverse_rms).astype(jnp.bfloat16)
        pre_act = jnp.dot(normed.reshape(-1, D).astype(jnp.float32), expanded_list[layer], precision=highest).reshape(hidden.shape)
        saved.append((hidden, normed, pre_act))
        hidden = (as_float + jax.nn.silu(pre_act)).astype(jnp.bfloat16)
    arriving = cotangent
    grads = [None] * LAYERS
    for layer in reversed(range(LAYERS)):
        entering, normed, pre_act = saved[layer]
        as_float = entering.astype(jnp.float32)
        inverse_rms = lax.rsqrt(lax.optimization_barrier(jnp.mean(as_float * as_float, axis=-1, keepdims=True)) + 1e-05)
        sigmoid_z = jax.nn.sigmoid(pre_act)
        grad_pre = (arriving.astype(jnp.float32) * (sigmoid_z * (1.0 + pre_act * (1.0 - sigmoid_z)))).astype(jnp.bfloat16)
        grad_normed = jnp.dot(grad_pre.reshape(-1, D).astype(jnp.float32), expanded_list[layer].T, precision=highest).reshape(entering.shape)
        scaled = as_float * inverse_rms
        arriving = (arriving.astype(jnp.float32) + inverse_rms * (grad_normed - scaled * lax.optimization_barrier(jnp.mean(grad_normed * scaled, axis=-1, keepdims=True)))).astype(jnp.bfloat16)
        grads[layer] = weight_grad(normed, grad_pre, live_rows[layer])
    rate = 0.1 / math.sqrt(LIVE * BLOCK)
    new_weights, new_moment, new_second = ([], [], [])
    for layer in range(LAYERS):
        gradient = grads[layer]
        moment_new = 0.9 * moment[layer] + 0.1 * gradient
        second_new = 0.95 * second[layer] + 0.05 * gradient * gradient
        stepped = weights[layer].astype(jnp.float32) - rate * moment_new / (jnp.sqrt(second_new) + 1e-08)
        new_weights.append(tree_prox(stepped, live_rows[layer]))
        new_moment.append(moment_new)
        new_second.append(second_new)
    return (jnp.stack(new_weights), jnp.stack(new_moment), jnp.stack(new_second))
```

```python
import functools
import math

import jax
import jax.numpy as jnp
from jax import lax
from jax.experimental import pallas as pl
from jax.experimental.pallas import tpu as pltpu
from jax.sharding import PartitionSpec as P

HEAD = 128
F32 = jnp.float32
BF16 = jnp.bfloat16
PAD = 16
TILE = 4
VMEM = pl.BlockSpec(memory_space=pltpu.VMEM)
SMEM = pl.BlockSpec(memory_space=pltpu.SMEM)
ANY = pl.BlockSpec(memory_space=pl.ANY)


def shrink(magnitude, threshold):
    return jnp.maximum(magnitude - threshold, 0.0) / jnp.maximum(magnitude, threshold)


def weight_copies(scal, sources, buffer, sems):
    half = buffer.shape[0] // 4
    waits = []
    for group in range(4):
        owner, part = group // 2, group % 2
        target = buffer.at[pl.ds(group * half, half)]
        candidates = sources[owner][part]
        for index, source in enumerate(candidates):

            @pl.when(scal[2 + part] == index)
            def _(source=source, target=target, group=group):
                pltpu.make_async_copy(source, target, sems.at[group]).start()

        waits.append(pltpu.make_async_copy(candidates[0], target, sems.at[group]).wait)
    return waits


def weight_sources(refs):
    sources = []
    for owner in range(2):
        own, x1, x2, x3, y1, y2, y3 = refs[owner * 7 : owner * 7 + 7]
        half = own.shape[0] // 2
        sources.append(
            (
                (own.at[pl.ds(0, half)], x1, y2, y3),
                (own.at[pl.ds(half, half)], x2, x3, y1),
            )
        )
    return sources


def column_loop(scal, half, columns, body, waits):
    for group in range(4):
        waits[group]()
        owner, part = group // 2, group % 2
        first = ((scal[1] + owner) % 2) * (2 * half) + part * half

        @pl.loop(0, half)
        def _(step, group=group, first=first):
            body(group * half + step, first + step, scal[0] * columns + first + step)


def forward_kernel(ways, whole, last, scal, live, *refs):
    count = 1 if whole else ways
    shards, refs = refs[:count], refs[count:]
    sources, refs = weight_sources(refs[:14]), refs[14:]
    outs = 3 if last else 4
    outputs, (buffer, sems) = refs[:outs], refs[outs:]
    z_ref, u_ref, r_ref = outputs[:3]
    waits = weight_copies(scal, sources, buffer, sems)
    features, tokens = u_ref.shape
    rows = z_ref.shape[0]
    block = buffer.shape[1]
    live_count = buffer.shape[2] // block
    total = jnp.zeros((1, tokens), F32)
    for shard in shards:
        value = shard[...].astype(F32)
        total = total + jnp.sum(value * value, axis=0, keepdims=True)
    inverse = lax.rsqrt(total * (1.0 / features) + 1e-05)
    r_ref[...] = jnp.broadcast_to(inverse, r_ref.shape)
    if whole:
        u_ref[...] = (shards[0][...].astype(F32) * inverse).astype(BF16)
    else:
        for step, shard in enumerate(shards):
            u_ref[pl.ds((scal[0] ^ step) * rows, rows), :] = (
                shard[...].astype(F32) * inverse
            ).astype(BF16)

    def column(slot, local, column_index):
        acc = jnp.zeros((block, tokens), F32)
        for tile in range(live_count // TILE):
            picked = jnp.concatenate(
                [
                    u_ref[pl.ds(live[column_index, tile * TILE + i] * block, block), :]
                    for i in range(TILE)
                ],
                axis=0,
            )
            acc = acc + jnp.dot(
                buffer[slot, :, pl.ds(tile * TILE * block, TILE * block)],
                picked,
                preferred_element_type=F32,
            )
        z_ref[pl.ds(local * block, block), :] = acc

    column_loop(scal, buffer.shape[0] // 4, rows // block, column, waits)
    if not last:
        own = shards[0][pl.ds(scal[0] * rows, rows), :] if whole else shards[0][...]
        pre = z_ref[...]
        outputs[3][...] = (own.astype(F32) + pre * jax.nn.sigmoid(pre)).astype(BF16)


def backward_kernel(ways, first, last, scal, live, *refs):
    if first:
        arriving_ref, refs = refs[0], refs[1:]
    else:
        older_ref, h_ref, r_ref = refs[:3]
        shares, refs = refs[3 : 3 + ways], refs[3 + ways :]
    pre_ref, refs = refs[0], refs[1:]
    if not last:
        sources, refs = weight_sources(refs[:14]), refs[14:]
    gz_ref, refs = refs[0], refs[1:]
    if not last:
        outgoing, refs = refs[:ways], refs[ways:]
    if not first:
        g_ref, refs = refs[0], refs[1:]
    rows, tokens = gz_ref.shape
    if not last:
        buffer, sems, du_ref = refs
        waits = weight_copies(scal, sources, buffer, sems)
    if first:
        arriving = arriving_ref[...].astype(F32)
    else:
        total = shares[0][pl.ds(0, rows), :].astype(F32)
        means = shares[0][pl.ds(rows, PAD), :].astype(F32)
        for share in shares[1:]:
            total = total + share[pl.ds(0, rows), :].astype(F32)
            means = means + share[pl.ds(rows, PAD), :].astype(F32)
        mean = jnp.sum(means, axis=0, keepdims=True) * (1.0 / (rows * ways))
        inverse = r_ref[0:1, :]
        scaled = h_ref[...].astype(F32) * inverse
        arriving = (older_ref[...].astype(F32) + inverse * (total - scaled * mean)).astype(BF16)
        g_ref[...] = arriving
        arriving = arriving.astype(F32)
    pre = pre_ref[...]
    sigmoid = jax.nn.sigmoid(pre)
    gz = (arriving * (sigmoid * (1.0 + pre * (1.0 - sigmoid)))).astype(BF16)
    gz_ref[...] = gz
    if last:
        return
    share = jnp.sum(gz.astype(F32) * pre, axis=0, keepdims=True)
    high = share.astype(BF16).astype(F32)
    low = share - high
    row = lax.broadcasted_iota(jnp.int32, (PAD, tokens), 0)
    extra = jnp.where(row == 0, high, jnp.where(row == 1, low, 0.0)).astype(BF16)
    du_ref[...] = jnp.zeros_like(du_ref)
    block = buffer.shape[1]
    live_count = buffer.shape[2] // block

    def column(slot, local, column_index):
        gz_block = gz_ref[pl.ds(local * block, block), :]
        for tile in range(live_count // TILE):
            product = lax.dot_general(
                buffer[slot, :, pl.ds(tile * TILE * block, TILE * block)],
                gz_block,
                (((0,), (0,)), ((), ())),
                preferred_element_type=F32,
            )
            for i in range(TILE):
                at = pl.ds(live[column_index, tile * TILE + i] * block, block)
                du_ref[at, :] += product[i * block : (i + 1) * block]

    column_loop(scal, buffer.shape[0] // 4, rows // block, column, waits)
    for step in range(ways):
        outgoing[step][pl.ds(0, rows), :] = du_ref[
            pl.ds((scal[0] ^ step) * rows, rows), :
        ].astype(BF16)
        outgoing[step][pl.ds(rows, PAD), :] = extra


def segment_sum(row, width):
    lanes = row.shape[-1]
    lane = lax.broadcasted_iota(jnp.int32, row.shape, row.ndim - 1)
    step = 1
    while step < width:
        ahead = pltpu.roll(row, lanes - step, row.ndim - 1)
        behind = pltpu.roll(row, step, row.ndim - 1)
        row = row + jnp.where((lane // step) % 2 == 0, ahead, behind)
        step *= 2
    return row


def update_kernel(chunks, inverse_tokens, first_column, live, *refs):
    gz_refs, u_refs, refs = refs[:chunks], refs[chunks : 2 * chunks], refs[2 * chunks :]
    weight_ref, moment_ref, second_ref = refs[:3]
    moment_out, second_out, stepped_ref, factor_ref, squares_ref = refs[3:]
    column = pl.program_id(0)
    column_index = first_column[0] + column
    block, wide = weight_ref.shape[1:]
    live_count = wide // block
    rate = 0.1 / math.sqrt(wide)
    lhs = jnp.concatenate([gz[...] for gz in gz_refs], axis=1)
    for tile in range(live_count // TILE):
        picked = jnp.concatenate(
            [
                jnp.concatenate(
                    [
                        u[pl.ds(live[column_index, tile * TILE + i] * block, block), :]
                        for u in u_refs
                    ],
                    axis=1,
                )
                for i in range(TILE)
            ],
            axis=0,
        )
        gradient = (
            lax.dot_general(
                lhs, picked, (((1,), (1,)), ((), ())), preferred_element_type=F32
            )
            * inverse_tokens
        )
        at = pl.ds(tile * TILE * block, TILE * block)
        moment = 0.9 * moment_ref[0, :, at] + 0.1 * gradient
        second = 0.95 * second_ref[0, :, at] + 0.05 * gradient * gradient
        stepped = weight_ref[0, :, at].astype(F32) - rate * moment / (jnp.sqrt(second) + 1e-08)
        moment_out[0, :, at] = moment
        second_out[0, :, at] = second
        stepped_ref[0, :, at] = stepped
        squares = segment_sum(jnp.sum(stepped * stepped, axis=0, keepdims=True), block)
        factor = shrink(jnp.sqrt(squares), 0.15 * math.sqrt(block / live_count))
        factor_ref[0, :, at] = factor
        squares_ref[0, :, at] = factor * factor * squares


def kernel_call(kernel, name, outs, in_specs, out_specs, limit_mib, **kwargs):
    return pl.pallas_call(
        kernel,
        out_shape=outs,
        in_specs=in_specs,
        out_specs=out_specs,
        compiler_params=pltpu.CompilerParams(vmem_limit_bytes=limit_mib << 20),
        name=name,
        **kwargs,
    )


def after(value, *others):
    return lax.optimization_barrier((value, *others))[0]


def local(x_in, cotangent, weights, live_rows, moment, second):
    sections = lax.axis_size("pipe")
    devices = lax.axis_size("dp")
    ways = devices // 2
    section = lax.axis_index("pipe")
    place = lax.axis_index("dp")
    line, core = (place // 2, place % 2)
    micro_count, share, features = x_in.shape
    own_columns, block, wide = weights.shape[1:]
    live_count = wide // block
    half = own_columns // 2
    columns = 2 * own_columns
    rows = columns * block
    tokens = ways * share
    column_count = live_rows.shape[1]

    def to_pipe(value, step):
        return lax.ppermute(value, "pipe", [(i, i ^ step) for i in range(sections)])

    def to_line(value, step):
        return lax.ppermute(value, "dp", [(i, i ^ (2 * step)) for i in range(devices)])

    def to_core(value):
        return lax.ppermute(value, "dp", [(i, i ^ 1) for i in range(devices)])

    own_live = live_rows[0]
    by_step = [own_live] + [to_pipe(own_live, step) for step in range(1, sections)]
    live = [lax.select_n(section ^ layer, *by_step) for layer in range(sections)]

    own = weights[0]
    first_half, second_half = own[:half], own[half:]
    x1 = to_pipe(first_half, 1)
    y1 = to_pipe(second_half, 2)
    x2 = to_pipe(jnp.where(section == 2, y1, second_half), 1)
    y2 = to_pipe(jnp.where(section == 1, x1, first_half), 2)
    x3 = to_pipe(after(jnp.where(section == 2, second_half, y1), x2), 1)
    y3 = to_pipe(after(jnp.where(section == 1, first_half, x1), y2), 2)
    mine = [own, x1, x2, x3, y1, y2, y3]
    siblings = [to_core(value) for value in mine]
    odd = (section == sections - 1).astype(jnp.int32)
    scal, held = [], []
    for layer in range(sections):
        step = section ^ layer
        source_first = jnp.where(step < 2, step, (step - 2) ^ odd + 0)
        source_first = jnp.where(step < 2, step, 2 + ((step - 2) ^ odd))
        source_second = jnp.where(
            step == 0, 0, jnp.where(step == 2, 3, 1 + ((step == 3).astype(jnp.int32) ^ odd))
        )
        scal.append(jnp.stack([line, core, source_first, source_second]).astype(jnp.int32))
        if layer == 0:
            pick = [0, 1, 2, 2, 4, 5, 5]
        else:
            pick = [0, 1, 2, 3, 4, 5, 6]
        held.append([mine[i] for i in pick] + [siblings[i] for i in pick])

    x_own = lax.dynamic_index_in_dim(x_in, section, 0, keepdims=False)
    cot_own = lax.dynamic_index_in_dim(cotangent, section, 0, keepdims=False)
    x_all = jnp.zeros((ways, share, features), BF16)
    cot_all = jnp.zeros((ways, share, rows), BF16)
    for step in range(ways):
        x_part = x_own if step == 0 else to_line(x_own, step)
        x_all = lax.dynamic_update_index_in_dim(x_all, x_part, line ^ step, 0)
        cot_part = lax.dynamic_slice_in_dim(cot_own, (line ^ step) * rows, rows, 1)
        cot_part = cot_part if step == 0 else to_line(cot_part, step)
        cot_all = lax.dynamic_update_index_in_dim(cot_all, cot_part, line ^ step, 0)
    x_all = x_all.reshape(tokens, features).T
    cot_all = cot_all.reshape(tokens, rows).T

    def sds(shape, dtype):
        return jax.ShapeDtypeStruct(shape, dtype)

    weight_scratch = [
        pltpu.VMEM((columns, block, wide), BF16),
        pltpu.SemaphoreType.DMA((4,)),
    ]
    limit = 48
    shards = [x_all]
    entering, inverses, normed, pre_acts = [None], [], [], []
    for layer in range(sections):
        last = layer == sections - 1
        outs = [
            sds((rows, tokens), F32),
            sds((features, tokens), BF16),
            sds((8, tokens), F32),
        ] + ([] if last else [sds((rows, tokens), BF16)])
        result = kernel_call(
            functools.partial(forward_kernel, ways, layer == 0, last),
            f"forward{layer}",
            outs,
            [SMEM, SMEM] + [VMEM] * len(shards) + [ANY] * 14,
            [VMEM] * len(outs),
            limit,
            scratch_shapes=weight_scratch,
        )(scal[layer], live[layer], *shards, *held[layer])
        pre_acts.append(result[0])
        normed.append(result[1])
        inverses.append(result[2])
        if not last:
            entering.append(result[3])
            shards = [result[3]] + [to_line(result[3], step) for step in range(1, ways)]

    u_chunks = [lax.select_n(section, *normed)]
    for step in range(1, sections):
        u_chunks.append(to_pipe(lax.select_n(section ^ step, *normed), step))
    u_chunks = u_chunks + [to_core(value) for value in u_chunks]

    gradients = [None] * sections
    arriving = [cot_all]
    for layer in reversed(range(sections)):
        first, last = layer == sections - 1, layer == 0
        outs = [sds((rows, tokens), BF16)]
        if not last:
            outs += [sds((rows + PAD, tokens), BF16)] * ways
        if not first:
            outs += [sds((rows, tokens), BF16)]
        operands = arriving + [pre_acts[layer]]
        weight_operands = [] if last else held[layer]
        result = kernel_call(
            functools.partial(backward_kernel, ways, first, last),
            f"backward{layer}",
            outs,
            [SMEM, SMEM] + [VMEM] * len(operands) + [ANY] * len(weight_operands),
            [VMEM] * len(outs),
            limit,
            scratch_shapes=[]
            if last
            else weight_scratch + [pltpu.VMEM((features, tokens), F32)],
        )(scal[layer], live[layer], *operands, *weight_operands)
        gradients[layer] = result[0]
        if not last:
            outgoing = result[1 : 1 + ways]
            incoming = [outgoing[0]] + [to_line(outgoing[k], k) for k in range(1, ways)]
            older = cot_all if first else result[1 + ways]
            arriving = [older, entering[layer], inverses[layer]] + incoming

    own_rows = own_columns * block
    gz_chunks = []
    for flip in range(2):
        for step in range(sections):
            value = lax.select_n(section ^ step, *gradients)
            value = lax.dynamic_slice_in_dim(value, (core ^ flip) * own_rows, own_rows, 0)
            if step or flip:
                value = lax.ppermute(
                    value,
                    ("pipe", "dp"),
                    [
                        (i * devices + j, (i ^ step) * devices + (j ^ flip))
                        for i in range(sections)
                        for j in range(devices)
                    ],
                )
            gz_chunks.append(value)

    chunks = len(gz_chunks)
    all_tokens = micro_count * devices * share
    per_column = pl.BlockSpec((1, block, wide), lambda j: (j, 0, 0))
    per_row = pl.BlockSpec((1, 1, wide), lambda j: (j, 0, 0))
    held_whole = pl.BlockSpec(
        (features, tokens), lambda j: (0, 0), pipeline_mode=pl.Buffered(1)
    )
    moment_new, second_new, stepped, factor, squares = kernel_call(
        functools.partial(update_kernel, chunks, 1.0 / all_tokens),
        "update",
        [sds((own_columns, block, wide), F32)] * 3 + [sds((own_columns, 1, wide), F32)] * 2,
        [SMEM, SMEM]
        + [pl.BlockSpec((block, tokens), lambda j: (j, 0))] * chunks
        + [held_whole] * chunks
        + [per_column] * 3,
        [per_column] * 3 + [per_row] * 2,
        56,
        grid=(own_columns,),
    )(
        jnp.stack([place * own_columns]).astype(jnp.int32),
        own_live,
        *gz_chunks,
        *u_chunks,
        own,
        moment[0],
        second[0],
    )
    own_index = lax.dynamic_slice_in_dim(own_live, place * own_columns, own_columns, 0)
    head_count = features // HEAD
    onehot = (
        (own_index // (HEAD // block))[:, :, None]
        == jnp.arange(head_count, dtype=jnp.int32)[None, None, :]
    ).astype(F32)
    leaf_squares = squares.reshape(own_columns, live_count, block)[:, :, 0]
    leaf_factor = factor.reshape(own_columns, live_count, block)[:, :, 0]
    head_share = jnp.sum(onehot * leaf_squares[:, :, None], axis=(0, 1))
    head_squares = head_share
    for step in range(1, devices):
        head_squares = head_squares + lax.ppermute(
            head_share, "dp", [(i, i ^ step) for i in range(devices)]
        )
    head_factor = shrink(jnp.sqrt(head_squares), 0.45 * math.sqrt(HEAD))
    layer_squares = jnp.sum(head_factor * head_factor * head_squares)
    layer_factor = shrink(jnp.sqrt(layer_squares), 0.45 * math.sqrt(features))
    scale = leaf_factor * jnp.sum(onehot * head_factor[None, None, :], axis=2) * layer_factor
    scale = jnp.broadcast_to(scale[:, :, None], (own_columns, live_count, block))
    weights_out = (stepped * scale.reshape(own_columns, 1, wide)).astype(BF16)
    return (weights_out[None], moment_new[None], second_new[None])


def solution(mesh):
    placed = (
        P(None, "dp", None),
        P(None, "dp", None),
        P("pipe", "dp", None, None),
        P("pipe", None, None),
        P("pipe", "dp", None, None),
        P("pipe", "dp", None, None),
    )
    return jax.shard_map(
        local,
        mesh=mesh,
        in_specs=placed,
        out_specs=(
            P("pipe", "dp", None, None),
            P("pipe", "dp", None, None),
            P("pipe", "dp", None, None),
        ),
        check_vma=False,
    )
```

```python
import functools
import math

import jax
import jax.numpy as jnp
from jax import lax
from jax.experimental import pallas as pl
from jax.experimental.pallas import tpu as pltpu
from jax.sharding import PartitionSpec as P

HEAD = 128
F32 = jnp.float32
BF16 = jnp.bfloat16
PAD = 16
LIMIT = 60
TILE = 4
VMEM = pl.BlockSpec(memory_space=pltpu.VMEM)
SMEM = pl.BlockSpec(memory_space=pltpu.SMEM)
ANY = pl.BlockSpec(memory_space=pl.ANY)


def shrink(magnitude, threshold):
    return jnp.maximum(magnitude - threshold, 0.0) / jnp.maximum(magnitude, threshold)


HOLDS = (
    ("own own", "x1 x2", "y2 y1", "y2 x2"),
    ("x1 x2", "own own", "y3 x3", "y3 y1"),
    ("y2 y1", "y3 x3", "own own", "x1 x3"),
    ("y3 x3", "y2 y1", "x1 x2", "own own"),
)


def holders(layer):
    names = sorted({name for row in HOLDS[layer] for name in row.split()})
    names.remove("own")
    return ["own"] + names


HEADER = 128


def live_row(table, layer, column, number, shape):
    return table[HEADER + (layer * shape[0] + column) * shape[1] + number]


def pick_kernel(layer_round, height, section, own, x1, y1, x_out, y_out, sems):
    half = pl.ds(0, height)
    cases = (
        (x_out.at[half], own.at[pl.ds(height, height)], y1.at[half], 2),
        (y_out.at[half], own.at[half], x1.at[half], 1),
    )
    for number, (out, mine, received, place) in enumerate(cases):
        passes = (section[0] == place) == (layer_round == 2)

        @pl.when(passes)
        def _(out=out, received=received, number=number):
            pltpu.make_async_copy(received, out, sems.at[number]).start()

        @pl.when(jnp.logical_not(passes))
        def _(out=out, mine=mine, number=number):
            pltpu.make_async_copy(mine, out, sems.at[number]).start()

    if layer_round == 2:
        extra = pl.ds(height, PAD)
        pltpu.make_async_copy(y1.at[extra], x_out.at[extra], sems.at[2]).start()
        pltpu.make_async_copy(y1.at[extra], x_out.at[extra], sems.at[2]).wait()
    for number, (out, _, received, _) in enumerate(cases):
        pltpu.make_async_copy(received, out, sems.at[number]).wait()


def weight_copies(layer, table, refs, buffer, sems):
    names = holders(layer)
    height = buffer.shape[0] // 8
    for group in range(8):
        owner, quarter = group // 4, group % 4
        held = dict(zip(names, refs[owner * len(names) : (owner + 1) * len(names)]))
        target = buffer.at[pl.ds(group * height, height)]
        for section, row in enumerate(HOLDS[layer]):
            name = row.split()[quarter // 2]
            first = quarter if name == "own" else quarter % 2
            source = held[name].at[pl.ds(first * height, height)]

            @pl.when(table[2] == section)
            def _(source=source, target=target, group=group):
                pltpu.make_async_copy(source, target, sems.at[group]).start()

    def wait(group):
        target = buffer.at[pl.ds(group * height, height)]
        pltpu.make_async_copy(refs[0].at[pl.ds(0, height)], target, sems.at[group]).wait()

    return wait


def column_loop(scal, own_columns, body, wait):
    taken, count = max(1, 4 // own_columns), max(1, own_columns // 4)

    @pl.loop(0, 8 // taken)
    def _(turn):
        for i in range(taken):
            wait(turn * taken + i)
        for i in range(count):
            slot = turn * count + i
            local = slot ^ (scal[1] * own_columns)
            body(slot, local, scal[0] * 2 * own_columns + local)


def forward_kernel(layer, ways, last, live_shape, scal, *refs):
    whole = layer == 0
    count = 1 if whole else ways
    shards, refs = refs[:count], refs[count:]
    held = 2 * len(holders(layer))
    weight_refs, refs = refs[:held], refs[held:]
    if not whole:
        refs = refs[len(HOLDS) :]
    outs = 2 if last else 3
    outputs, refs = refs[:outs], refs[outs:]
    sends, refs = refs[: len(HOLDS)], refs[len(HOLDS) :]
    buffer, u_ref, sems, send_sem = refs
    z_ref, r_ref = outputs[:2]
    wait = weight_copies(layer, scal, weight_refs, buffer, sems)
    features, tokens = u_ref.shape
    rows = z_ref.shape[0]
    live_count = live_shape[1]
    block = buffer.shape[1] // live_count
    total = jnp.zeros((1, tokens), F32)
    for shard in shards:
        value = shard[...].astype(F32)
        total = total + jnp.sum(value * value, axis=0, keepdims=True)
    inverse = lax.rsqrt(total * (1.0 / features) + 1e-05)
    r_ref[...] = jnp.broadcast_to(inverse, r_ref.shape)
    if whole:
        u_ref[...] = (shards[0][...].astype(F32) * inverse).astype(BF16)
    else:
        for step, shard in enumerate(shards):
            u_ref[pl.ds((scal[0] ^ step) * rows, rows), :] = (
                shard[...].astype(F32) * inverse
            ).astype(BF16)
    for step, send in enumerate(sends):

        @pl.when((scal[2] ^ step) == layer)
        def _(send=send):
            pltpu.make_async_copy(u_ref, send, send_sem.at[0]).start()

    width = TILE * block
    tiles = live_count // TILE

    def picked(column_index, tile):
        return jnp.concatenate(
            [
                u_ref[
                    pl.ds(
                        live_row(scal, layer, column_index, tile * TILE + i, live_shape) * block,
                        block,
                    ),
                    :,
                ]
                for i in range(TILE)
            ],
            axis=0,
        )

    def column(slot, local, column_index):
        acc = jnp.zeros((2 * block, 2 * tokens), F32)
        at = pl.ds(slot * block, block)
        for tile in range(tiles // 2):
            other = tile + tiles // 2
            lhs = jnp.concatenate(
                [
                    buffer[at, pl.ds(tile * width, width)],
                    buffer[at, pl.ds(other * width, width)],
                ],
                axis=0,
            )
            rhs = jnp.concatenate(
                [picked(column_index, tile), picked(column_index, other)], axis=1
            )
            acc = acc + jnp.dot(lhs, rhs, preferred_element_type=F32)
        z_ref[pl.ds(local * block, block), :] = acc[:block, :tokens] + acc[block:, tokens:]

    column_loop(scal, rows // block // 2, column, wait)
    pltpu.make_async_copy(u_ref, sends[0], send_sem.at[0]).wait()
    if not last:
        own = shards[0][pl.ds(scal[0] * rows, rows), :] if whole else shards[0][...]
        pre = z_ref[...]
        outputs[2][...] = (own.astype(F32) + pre * jax.nn.sigmoid(pre)).astype(BF16)


def backward_kernel(layer, ways, live_shape, scal, *refs):
    first, last = layer == len(HOLDS) - 1, layer == 0
    if first:
        arriving_ref, refs = refs[0], refs[1:]
    else:
        older_ref, h_ref, r_ref = refs[:3]
        shares, refs = refs[3 : 3 + ways], refs[3 + ways :]
    pre_ref, refs = refs[0], refs[1:]
    if last:
        others, refs = refs[: len(HOLDS) - 1], refs[len(HOLDS) - 1 :]
        sorted_refs, (gz_ref,) = refs[:-1], refs[-1:]
    else:
        held = 2 * len(holders(layer))
        weight_refs, refs = refs[:held], refs[held:]
        gz_ref, refs = refs[0], refs[1:]
        outgoing, refs = refs[:ways], refs[ways:]
        if not first:
            g_ref, refs = refs[0], refs[1:]
        buffer, sems, du_ref = refs
        wait = weight_copies(layer, scal, weight_refs, buffer, sems)
    rows, tokens = gz_ref.shape
    if first:
        arriving = arriving_ref[...].astype(F32)
    else:
        total = shares[0][pl.ds(0, rows), :].astype(F32)
        means = shares[0][pl.ds(rows, PAD), :].astype(F32)
        for share in shares[1:]:
            total = total + share[pl.ds(0, rows), :].astype(F32)
            means = means + share[pl.ds(rows, PAD), :].astype(F32)
        mean = jnp.sum(means, axis=0, keepdims=True) * (1.0 / (rows * ways))
        inverse = r_ref[0:1, :]
        scaled = h_ref[...].astype(F32) * inverse
        arriving = (older_ref[...].astype(F32) + inverse * (total - scaled * mean)).astype(BF16)
        if not last:
            g_ref[...] = arriving
        arriving = arriving.astype(F32)
    pre = pre_ref[...]
    sigmoid = jax.nn.sigmoid(pre)
    gz = (arriving * (sigmoid * (1.0 + pre * (1.0 - sigmoid)))).astype(BF16)
    gz_ref[...] = gz
    if last:
        half = rows // 2
        for step in range(len(HOLDS)):
            for number, source in enumerate((gz_ref, *others)):

                @pl.when((scal[2] ^ step) == number)
                def _(step=step, source=source):
                    for flip in range(2):
                        sorted_refs[2 * step + flip][...] = source[
                            pl.ds((scal[1] ^ flip) * half, half), :
                        ]

        return
    share = jnp.sum(gz.astype(F32) * pre, axis=0, keepdims=True)
    high = share.astype(BF16).astype(F32)
    low = share - high
    row = lax.broadcasted_iota(jnp.int32, (PAD, tokens), 0)
    extra = jnp.where(row == 0, high, jnp.where(row == 1, low, 0.0)).astype(BF16)
    du_ref[...] = jnp.zeros_like(du_ref)
    live_count = live_shape[1]
    block = buffer.shape[1] // live_count

    width = TILE * block
    tiles = live_count // TILE

    def column(slot, local, column_index):
        gz_block = gz_ref[pl.ds(local * block, block), :]
        empty = jnp.zeros_like(gz_block)
        rhs = jnp.concatenate(
            [
                jnp.concatenate([gz_block, empty], axis=1),
                jnp.concatenate([empty, gz_block], axis=1),
            ],
            axis=0,
        )
        at = pl.ds(slot * block, block)
        for tile in range(tiles // 2):
            other = tile + tiles // 2
            lhs = jnp.concatenate(
                [
                    buffer[at, pl.ds(tile * width, width)],
                    buffer[at, pl.ds(other * width, width)],
                ],
                axis=0,
            )
            product = lax.dot_general(
                lhs, rhs, (((0,), (0,)), ((), ())), preferred_element_type=F32
            )
            for side, first_block in enumerate((tile * TILE, other * TILE)):
                for i in range(TILE):
                    row = live_row(scal, layer, column_index, first_block + i, live_shape)
                    du_ref[pl.ds(row * block, block), :] += product[
                        i * block : (i + 1) * block, side * tokens : (side + 1) * tokens
                    ]

    column_loop(scal, rows // block // 2, column, wait)
    for step in range(ways):
        outgoing[step][pl.ds(0, rows), :] = du_ref[
            pl.ds((scal[0] ^ step) * rows, rows), :
        ].astype(BF16)
        outgoing[step][pl.ds(rows, PAD), :] = extra


def segment_sum(row, width):
    lanes = row.shape[-1]
    lane = lax.broadcasted_iota(jnp.int32, row.shape, row.ndim - 1)
    step = 1
    while step < width:
        ahead = pltpu.roll(row, lanes - step, row.ndim - 1)
        behind = pltpu.roll(row, step, row.ndim - 1)
        row = row + jnp.where((lane // step) % 2 == 0, ahead, behind)
        step *= 2
    return row


def update_kernel(chunks, inverse_tokens, live_shape, table, *refs):
    gz_refs, u_refs, refs = refs[:chunks], refs[chunks : 2 * chunks], refs[2 * chunks :]
    weight_ref, moment_ref, second_ref, head_ref = refs[:4]
    moment_out, second_out, stepped_ref, factor_ref, heads_ref, square_ref = refs[4:]
    column = pl.program_id(0)
    column_index = (table[0] * 2 + table[1]) * pl.num_programs(0) + column
    block, wide = weight_ref.shape[1:]
    live_count = wide // block
    rate = 0.1 / math.sqrt(wide)

    @pl.when(column == 0)
    def _():
        square_ref[...] = jnp.zeros_like(square_ref)

    lhs = jnp.concatenate([gz[...] for gz in gz_refs], axis=1)
    for tile in range(live_count // TILE):
        picked = jnp.concatenate(
            [
                jnp.concatenate(
                    [
                        u[
                            pl.ds(
                                live_row(
                                    table, table[2], column_index, tile * TILE + i, live_shape
                                )
                                * block,
                                block,
                            ),
                            :,
                        ]
                        for u in u_refs
                    ],
                    axis=1,
                )
                for i in range(TILE)
            ],
            axis=0,
        )
        gradient = (
            lax.dot_general(
                lhs, picked, (((1,), (1,)), ((), ())), preferred_element_type=F32
            )
            * inverse_tokens
        )
        at = pl.ds(tile * TILE * block, TILE * block)
        moment = 0.9 * moment_ref[0, :, at] + 0.1 * gradient
        second = 0.95 * second_ref[0, :, at] + 0.05 * gradient * gradient
        stepped = weight_ref[0, :, at].astype(F32) - rate * moment / (jnp.sqrt(second) + 1e-08)
        moment_out[0, :, at] = moment
        second_out[0, :, at] = second
        stepped_ref[0, :, at] = stepped
        square_ref[pl.ds(column, 1), at] = jnp.sum(stepped * stepped, axis=0, keepdims=True)

    @pl.when(column == pl.num_programs(0) - 1)
    def _():
        squares = segment_sum(square_ref[...], block)
        factor = shrink(jnp.sqrt(squares), 0.15 * math.sqrt(block / live_count))
        factor_ref[...] = factor
        leafed = factor * factor * squares * (1.0 / block)
        head = head_ref[...]
        lane = lax.broadcasted_iota(jnp.int32, heads_ref.shape, 1)
        heads = jnp.zeros(heads_ref.shape, F32)
        for number in range(live_shape[0] * block // HEAD):
            share = jnp.sum(jnp.where(head == number, leafed, 0.0), axis=0, keepdims=True)
            heads = jnp.where(lane == number, jnp.sum(share, axis=1, keepdims=True), heads)
        heads_ref[...] = heads


def output_kernel(parts, features, *refs):
    head_refs, refs = refs[:parts], refs[parts:]
    head_ref, factor_ref, stepped_ref, out_ref, scale_ref = refs
    column = pl.program_id(0)

    @pl.when(column == 0)
    def _():
        squares = head_refs[0][0:1, :]
        for ref in head_refs[1:]:
            squares = squares + ref[0:1, :]
        head_factor = shrink(jnp.sqrt(squares), 0.45 * math.sqrt(HEAD))
        layer = jnp.sum(head_factor * head_factor * squares, axis=1, keepdims=True)
        head_factor = head_factor * shrink(jnp.sqrt(layer), 0.45 * math.sqrt(features))
        head = head_ref[...]
        scale = jnp.zeros(head.shape, F32)
        for number in range(features // HEAD):
            scale = jnp.where(head == number, head_factor[:, number : number + 1], scale)
        scale_ref[...] = scale * factor_ref[...]

    out_ref[0] = (stepped_ref[0] * scale_ref[pl.ds(column, 1), :]).astype(BF16)


def kernel_call(kernel, name, outs, in_specs, out_specs, limit_mib, **kwargs):
    return pl.pallas_call(
        kernel,
        out_shape=outs,
        in_specs=in_specs,
        out_specs=out_specs,
        compiler_params=pltpu.CompilerParams(vmem_limit_bytes=limit_mib << 20),
        name=name,
        **kwargs,
    )


def after(value, *others):
    return lax.optimization_barrier((value, *others))[0]


def local(x_in, cotangent, weights, live_rows, moment, second):
    sections = lax.axis_size("pipe")
    devices = lax.axis_size("dp")
    ways = devices // 2
    section = lax.axis_index("pipe")
    place = lax.axis_index("dp")
    line, core = (place // 2, place % 2)
    micro_count, share, features = x_in.shape
    own_columns, block, wide = weights.shape[1:]
    columns = 2 * own_columns
    rows = columns * block
    tokens = ways * share

    def to_pipe(value, step):
        return lax.ppermute(value, "pipe", [(i, i ^ step) for i in range(sections)])

    def to_line(value, step):
        return lax.ppermute(value, "dp", [(i, i ^ (2 * step)) for i in range(devices)])

    def to_core(value):
        return lax.ppermute(value, "dp", [(i, i ^ 1) for i in range(devices)])

    own_live = live_rows[0]

    x_own = lax.dynamic_index_in_dim(x_in, section, 0, keepdims=False)
    own = weights[0].reshape(own_columns * block, wide)
    height = own_columns * block // 2
    extra = jnp.pad(own_live.reshape(1, wide).astype(BF16), ((0, PAD - 1), (0, 0)))
    half1 = jnp.concatenate([own[:height], extra], axis=0)
    half2 = jnp.concatenate([own[height:], extra], axis=0)

    def slot(x_value, y_value, *extra):
        return lax.optimization_barrier((to_pipe(x_value, 1), to_pipe(y_value, 2), *extra))

    def along(value, *deps):
        value = after(value, *deps) if deps else value
        return [to_line(value, step) for step in range(1, ways)]

    def pick(layer_round, first_source, second_source):
        return kernel_call(
            functools.partial(pick_kernel, layer_round, height),
            f"pick{layer_round}",
            [
                jax.ShapeDtypeStruct((height + (PAD if layer_round == 2 else 0), wide), BF16),
                jax.ShapeDtypeStruct((height, wide), BF16),
            ],
            [SMEM] + [ANY] * 3,
            [VMEM] * 2,
            LIMIT,
            scratch_shapes=[pltpu.SemaphoreType.DMA((3,))],
        )(jnp.stack([section]).astype(jnp.int32), own, first_source, second_source)

    x1, y1, *x_parts = slot(half1, half2, *along(x_own, half1, half2))
    x2, y2 = slot(*pick(2, x1, y1))
    by_step = [own_live] + [
        value[height].astype(jnp.int32).reshape(own_live.shape) for value in (x1, y1, x2)
    ]
    mine = dict(own=own, x1=x1, x2=x2, y1=y1, y2=y2)
    siblings = dict(own=to_core(after(own, x1, y1)))
    siblings.update({name: to_core(mine[name]) for name in ("x1", "y1", "x2", "y2")})
    x3, y3 = slot(*pick(3, x1, after(y1, x2, y2)))
    mine.update(x3=x3, y3=y3)
    live = [lax.select_n(section ^ layer, *by_step) for layer in range(sections)]
    live_shape = own_live.shape
    header = jnp.stack([line, core, section]).astype(jnp.int32)
    table = jnp.concatenate(
        [jnp.pad(header, (0, HEADER - header.shape[0]))] + [value.reshape(-1) for value in live]
    )

    def layer_weights(layer):
        names = holders(layer)
        return [mine[name] for name in names] + [siblings[name] for name in names]

    def sds(shape, dtype):
        return jax.ShapeDtypeStruct(shape, dtype)

    x_all = jnp.zeros((ways, share, features), BF16)
    for step, part in enumerate([x_own, *x_parts]):
        x_all = lax.dynamic_update_index_in_dim(x_all, part, line ^ step, 0)
    x_all = x_all.reshape(tokens, features).T

    weight_scratch = [pltpu.VMEM((columns * block, wide), BF16)]
    shards = [x_all]
    entering, inverses, pre_acts, sends = [None], [], [], []
    for layer in range(sections):
        last = layer == sections - 1
        outs = [sds((rows, tokens), F32), sds((8, tokens), F32)]
        outs += [] if last else [sds((rows, tokens), BF16)]
        plain = len(outs)
        outs += [sds((features, tokens), BF16)] * sections
        operands = layer_weights(layer)
        before = 1 + len(shards) + len(operands)
        result = kernel_call(
            functools.partial(forward_kernel, layer, ways, last, live_shape),
            f"forward{layer}",
            outs,
            [SMEM] + [VMEM] * len(shards) + [ANY] * (len(operands) + len(sends)),
            [VMEM] * plain + [ANY] * sections,
            LIMIT,
            scratch_shapes=weight_scratch
            + [
                pltpu.VMEM((features, tokens), BF16),
                pltpu.SemaphoreType.DMA((8,)),
                pltpu.SemaphoreType.DMA((1,)),
            ],
            input_output_aliases={before + i: plain + i for i in range(len(sends))},
        )(table, *shards, *operands, *sends)
        pre_acts.append(result[0])
        inverses.append(result[1])
        sends = result[plain:]
        if not last:
            entering.append(result[2])
            shards = [result[2]] + [to_line(result[2], step) for step in range(1, ways)]
            if layer == 0:
                for name in ("x3", "y3"):
                    siblings[name] = to_core(after(mine[name], *shards[1:]))

    cot_own = after(lax.dynamic_index_in_dim(cotangent, section, 0, keepdims=False), entering[2])
    cot_all = jnp.zeros((ways, share, rows), BF16)
    for step in range(ways):
        cot_part = lax.dynamic_slice_in_dim(cot_own, (line ^ step) * rows, rows, 1)
        cot_part = cot_part if step == 0 else to_line(cot_part, step)
        cot_all = lax.dynamic_update_index_in_dim(cot_all, cot_part, line ^ step, 0)
    cot_all = cot_all.reshape(tokens, rows).T

    u_chunks, u_siblings = [sends[0]] + [None] * (sections - 1), [None] * sections
    u_chunks[1], u_chunks[2] = (to_pipe(sends[1], 1), to_pipe(sends[2], 2))
    gradients = [None] * sections
    arriving = [cot_all]
    for layer in reversed(range(sections)):
        first, last = layer == sections - 1, layer == 0
        if last:
            outs = [sds((rows // 2, tokens), BF16)] * (2 * sections)
            operands = gradients[1:]
            specs, scratch = [VMEM] * len(operands), [pltpu.VMEM((rows, tokens), BF16)]
        else:
            outs = [sds((rows, tokens), BF16)]
            outs += [sds((rows + PAD, tokens), BF16)] * ways
            outs += [] if first else [sds((rows, tokens), BF16)]
            operands = layer_weights(layer)
            specs = [ANY] * len(operands)
            scratch = weight_scratch + [
                pltpu.SemaphoreType.DMA((8,)),
                pltpu.VMEM((features, tokens), F32),
            ]
        operands = arriving + [pre_acts[layer]] + operands
        result = kernel_call(
            functools.partial(backward_kernel, layer, ways, live_shape),
            f"backward{layer}",
            outs,
            [SMEM] + [VMEM] * (len(arriving) + 1) + specs,
            [VMEM] * len(outs),
            LIMIT,
            scratch_shapes=scratch,
        )(table, *operands)
        if last:
            break
        gradients[layer] = result[0]
        outgoing = result[1 : 1 + ways]
        incoming = [outgoing[0]] + [to_line(outgoing[k], k) for k in range(1, ways)]
        older = cot_all if first else result[1 + ways]
        if first:
            incoming[0] = after(incoming[0], u_chunks[1], u_chunks[2])
            u_chunks[3] = to_pipe(after(sends[3], *incoming), 3)
        elif layer == sections - 2:
            for number in (0, 1):
                u_siblings[number] = to_core(after(u_chunks[number], result[0]))
            incoming[0] = after(incoming[0], *u_siblings[:2])
        else:
            for number in (2, 3):
                u_siblings[number] = to_core(after(u_chunks[number], result[0]))
            incoming[0] = after(incoming[0], *u_siblings[2:])
        arriving = [older, entering[layer], inverses[layer]] + incoming
    u_chunks = u_chunks + u_siblings

    gz_chunks = [None] * (2 * sections)
    order = [(step, flip) for step in (3, 1, 2) for flip in range(2)] + [(0, 1), (0, 0)]
    for step, flip in order:
        value = result[2 * step + flip]
        if step or flip:
            value = lax.ppermute(
                value,
                ("pipe", "dp"),
                [
                    (i * devices + j, (i ^ step) * devices + (j ^ flip))
                    for i in range(sections)
                    for j in range(devices)
                ],
            )
        gz_chunks[flip * sections + step] = value

    chunks = len(gz_chunks)
    all_tokens = micro_count * devices * share
    padded = max(8, own_columns)
    own_index = lax.dynamic_slice_in_dim(own_live, place * own_columns, own_columns, 0)
    head = jnp.repeat(own_index // (HEAD // block), block, axis=1)
    head = jnp.concatenate([head, jnp.full((padded - own_columns, wide), -1, jnp.int32)], axis=0)
    per_column = pl.BlockSpec((1, block, wide), lambda j, *_: (j, 0, 0))
    per_lane = pl.BlockSpec((padded, wide), lambda j, *_: (0, 0))
    per_head = pl.BlockSpec((8, 128), lambda j, *_: (0, 0))
    held_whole = pl.BlockSpec(
        (features, tokens), lambda j, *_: (0, 0), pipeline_mode=pl.Buffered(1)
    )
    moment_new, second_new, stepped, factor, heads = pl.pallas_call(
        functools.partial(update_kernel, chunks, 1.0 / all_tokens, live_shape),
        out_shape=[sds((own_columns, block, wide), F32)] * 3
        + [sds((padded, wide), F32), sds((8, 128), F32)],
        grid_spec=pltpu.PrefetchScalarGridSpec(
            num_scalar_prefetch=1,
            grid=(own_columns,),
            in_specs=[pl.BlockSpec((block, tokens), lambda j, *_: (j, 0))] * chunks
            + [held_whole] * chunks
            + [per_column] * 3
            + [per_lane],
            out_specs=[per_column] * 3 + [per_lane, per_head],
            scratch_shapes=[pltpu.VMEM((padded, wide), F32)],
        ),
        compiler_params=pltpu.CompilerParams(vmem_limit_bytes=LIMIT << 20),
        name="update",
    )(
        table,
        *gz_chunks,
        *u_chunks,
        weights[0],
        moment[0],
        second[0],
        head,
    )
    heads = heads + to_core(heads)
    head_parts = [heads] + [to_line(heads, step) for step in range(1, ways)]
    weights_out = kernel_call(
        functools.partial(output_kernel, len(head_parts), features),
        "output",
        sds((own_columns, block, wide), BF16),
        [per_head] * len(head_parts) + [per_lane] * 2 + [per_column],
        per_column,
        LIMIT,
        grid=(own_columns,),
        scratch_shapes=[pltpu.VMEM((padded, wide), F32)],
    )(*head_parts, head, factor, stepped)
    return (weights_out[None], moment_new[None], second_new[None])


def solution(mesh):
    placed = (
        P(None, "dp", None),
        P(None, "dp", None),
        P("pipe", "dp", None, None),
        P("pipe", None, None),
        P("pipe", "dp", None, None),
        P("pipe", "dp", None, None),
    )
    return jax.shard_map(
        local,
        mesh=mesh,
        in_specs=placed,
        out_specs=(
            P("pipe", "dp", None, None),
            P("pipe", "dp", None, None),
            P("pipe", "dp", None, None),
        ),
        check_vma=False,
    )
```

```python
import functools
import math

import jax
import jax.numpy as jnp
from jax import lax
from jax.experimental import pallas as pl
from jax.experimental.pallas import tpu as pltpu
from jax.sharding import PartitionSpec as P

HEAD = 128
F32 = jnp.float32
BF16 = jnp.bfloat16
PAD = 16
LIMIT = 24
TILE = 4
VMEM = pl.BlockSpec(memory_space=pltpu.VMEM)
SMEM = pl.BlockSpec(memory_space=pltpu.SMEM)
HBM = pl.BlockSpec(memory_space=pltpu.HBM)


def shrink(magnitude, threshold):
    return jnp.maximum(magnitude - threshold, 0.0) / jnp.maximum(magnitude, threshold)


HOLDS = (
    ("own own", "x1 x2", "y2 y1", "y2 x2"),
    ("x1 x2", "own own", "y3 x3", "y3 y1"),
    ("y2 y1", "y3 x3", "own own", "x1 x3"),
    ("y3 x3", "y2 y1", "x1 x2", "own own"),
)


def holders(layer):
    names = sorted({name for row in HOLDS[layer] for name in row.split()})
    names.remove("own")
    return ["own"] + names


def turns(ways):
    return [0] + list(reversed(range(1, ways)))


def places():
    place = lax.axis_index("dp")
    return place // 2, place % 2, lax.axis_index("pipe")


def live_copy(layer, section, live_hbm, live, sem):
    count = live.shape[0]
    start = pl.multiple_of((section ^ layer) * count, count)
    return pltpu.make_async_copy(live_hbm.at[pl.ds(start, count)], live, sem)


def live_row(live, column, number, shape):
    return live[column * shape[1] + number]


def split_kernel(own, extra, first, second, sems):
    height = own.shape[0] // 2
    copies = []
    for number, out in enumerate((first, second)):
        half = own.at[pl.ds(number * height, height)]
        copies.append((half, out.at[pl.ds(0, height)], sems.at[2 * number]))
        copies.append((extra, out.at[pl.ds(height, PAD)], sems.at[2 * number + 1]))
    for source, target, sem in copies:
        pltpu.make_async_copy(source, target, sem).start()
    for source, target, sem in copies:
        pltpu.make_async_copy(source, target, sem).wait()


def pick_kernel(layer_round, height, own, x1, y1, x_out, y_out, sems):
    section = places()[2]
    half = pl.ds(0, height)
    cases = (
        (x_out.at[half], own.at[pl.ds(height, height)], y1.at[half], 2),
        (y_out.at[half], own.at[half], x1.at[half], 1),
    )
    for number, (out, mine, received, place) in enumerate(cases):
        passes = (section == place) == (layer_round == 2)

        @pl.when(passes)
        def _(out=out, received=received, number=number):
            pltpu.make_async_copy(received, out, sems.at[number]).start()

        @pl.when(jnp.logical_not(passes))
        def _(out=out, mine=mine, number=number):
            pltpu.make_async_copy(mine, out, sems.at[number]).start()

    if layer_round == 2:
        extra = pl.ds(height, PAD)
        pltpu.make_async_copy(y1.at[extra], x_out.at[extra], sems.at[2]).start()
        pltpu.make_async_copy(y1.at[extra], x_out.at[extra], sems.at[2]).wait()
    for number, (out, _, received, _) in enumerate(cases):
        pltpu.make_async_copy(received, out, sems.at[number]).wait()


def weight_copies(layer, section_here, refs, buffer, sems):
    names = holders(layer)
    height = buffer.shape[0] // 8
    for group in range(8):
        owner, quarter = group // 4, group % 4
        held = dict(zip(names, refs[owner * len(names) : (owner + 1) * len(names)]))
        target = buffer.at[pl.ds(group * height, height)]
        for section, row in enumerate(HOLDS[layer]):
            name = row.split()[quarter // 2]
            first = quarter if name == "own" else quarter % 2
            source = held[name].at[pl.ds(first * height, height)]

            @pl.when(section_here == section)
            def _(source=source, target=target, group=group):
                pltpu.make_async_copy(source, target, sems.at[group]).start()

    def wait(group):
        target = buffer.at[pl.ds(group * height, height)]
        pltpu.make_async_copy(refs[0].at[pl.ds(0, height)], target, sems.at[group]).wait()

    return wait


def load_kernel(layer, *refs):
    refs, (out, sems) = refs[:-2], refs[-2:]
    wait = weight_copies(layer, places()[2], refs, out, sems)
    for group in range(8):
        wait(group)


def gather_kernel(*refs):
    refs, (out, sems) = refs[:-2], refs[-2:]
    for number, ref in enumerate(refs):
        pltpu.make_async_copy(ref, out.at[number], sems.at[number]).start()
    for number, ref in enumerate(refs):
        pltpu.make_async_copy(ref, out.at[number], sems.at[number]).wait()


def column_loop(line, core, own_columns, body, wait):
    taken, count = max(1, 4 // own_columns), max(1, own_columns // 4)

    @pl.loop(0, 8 // taken)
    def _(turn):
        for i in range(taken if wait else 0):
            wait(turn * taken + i)
        for i in range(count):
            slot = turn * count + i
            local = slot ^ (core * own_columns)
            body(slot, local, line * 2 * own_columns + local)


def forward_kernel(layer, ways, live_shape, live_hbm, *refs):
    line, core, section = places()
    whole, last = layer == 0, layer == len(HOLDS) - 1
    count = 1 if whole else ways
    shards, refs = refs[:count], refs[count:]
    if last:
        arriving_ref, refs = refs[0], refs[1:]
    loaded = layer > 1
    held = 1 if loaded else 2 * len(holders(layer))
    weight_refs, refs = refs[:held], refs[held:]
    if not whole:
        refs = refs[len(HOLDS) :]
    outs = 2 + ways if last else 3
    outputs, refs = refs[:outs], refs[outs:]
    sends, refs = refs[: len(HOLDS)], refs[len(HOLDS) :]
    u_ref, send_sem, live, live_sem = refs[:4]
    refs = refs[4:]
    if loaded:
        buffer, wait = weight_refs[0], None
    else:
        (buffer, sems), refs = refs[:2], refs[2:]
        wait = weight_copies(layer, section, weight_refs, buffer, sems)
    live_copy(layer, section, live_hbm, live, live_sem.at[0]).start()
    r_ref = outputs[0]
    z_ref = refs[0] if last else outputs[1]
    features, tokens = u_ref.shape
    rows = z_ref.shape[0]
    live_count = live_shape[1]
    block = buffer.shape[1] // live_count
    total = jnp.zeros((1, tokens), F32)
    for shard in shards:
        value = shard[...].astype(F32)
        total = total + jnp.sum(value * value, axis=0, keepdims=True)
    inverse = lax.rsqrt(total * (1.0 / features) + 1e-05)
    r_ref[...] = jnp.broadcast_to(inverse, r_ref.shape)
    if whole:
        u_ref[...] = (shards[0][...].astype(F32) * inverse).astype(BF16)
    else:
        for step, shard in zip(turns(ways), shards):
            u_ref[pl.ds((line ^ step) * rows, rows), :] = (
                shard[...].astype(F32) * inverse
            ).astype(BF16)
    for step, send in enumerate(sends):

        @pl.when((section ^ step) == layer)
        def _(send=send):
            pltpu.make_async_copy(u_ref, send, send_sem.at[0]).start()

    width = TILE * block
    tiles = live_count // TILE
    live_copy(layer, section, live_hbm, live, live_sem.at[0]).wait()

    def picked(column_index, tile):
        return jnp.concatenate(
            [
                u_ref[
                    pl.ds(
                        live_row(live, column_index, tile * TILE + i, live_shape) * block,
                        block,
                    ),
                    :,
                ]
                for i in range(TILE)
            ],
            axis=0,
        )

    def column(slot, local, column_index):
        acc = jnp.zeros((2 * block, 2 * tokens), F32)
        at = pl.ds(slot * block, block)
        for tile in range(tiles // 2):
            other = tile + tiles // 2
            lhs = jnp.concatenate(
                [
                    buffer[at, pl.ds(tile * width, width)],
                    buffer[at, pl.ds(other * width, width)],
                ],
                axis=0,
            )
            rhs = jnp.concatenate(
                [picked(column_index, tile), picked(column_index, other)], axis=1
            )
            acc = acc + jnp.dot(lhs, rhs, preferred_element_type=F32)
        z_ref[pl.ds(local * block, block), :] = acc[:block, :tokens] + acc[block:, tokens:]

    column_loop(line, core, rows // block // 2, column, wait)
    if last:
        held_weights = (buffer, live, refs[1])
        backward_products(
            line, core, arriving_ref[...], z_ref[...], held_weights, live_shape, outputs[1], outputs[2:]
        )
    pltpu.make_async_copy(u_ref, sends[0], send_sem.at[0]).wait()
    if not last:
        own = shards[0][pl.ds(line * rows, rows), :] if whole else shards[0][...]
        pre = z_ref[...]
        outputs[2][...] = (own.astype(F32) + pre * jax.nn.sigmoid(pre)).astype(BF16)


def pre_gradient(arriving, pre):
    sigmoid = jax.nn.sigmoid(pre)
    return (arriving.astype(F32) * (sigmoid * (1.0 + pre * (1.0 - sigmoid)))).astype(BF16)


def backward_products(line, core, arriving, pre, held_weights, live_shape, gz_ref, outgoing):
    buffer, live, du_ref = held_weights
    rows, tokens = gz_ref.shape
    gz = pre_gradient(arriving, pre)
    gz_ref[...] = gz
    share = jnp.sum(gz.astype(F32) * pre, axis=0, keepdims=True)
    high = share.astype(BF16).astype(F32)
    low = share - high
    row = lax.broadcasted_iota(jnp.int32, (PAD, tokens), 0)
    extra = jnp.where(row == 0, high, jnp.where(row == 1, low, 0.0)).astype(BF16)
    du_ref[...] = jnp.zeros_like(du_ref)
    live_count = live_shape[1]
    block = buffer.shape[1] // live_count

    width = TILE * block
    tiles = live_count // TILE

    def column(slot, local, column_index):
        gz_block = gz_ref[pl.ds(local * block, block), :]
        empty = jnp.zeros_like(gz_block)
        rhs = jnp.concatenate(
            [
                jnp.concatenate([gz_block, empty], axis=1),
                jnp.concatenate([empty, gz_block], axis=1),
            ],
            axis=0,
        )
        at = pl.ds(slot * block, block)
        for tile in range(tiles // 2):
            other = tile + tiles // 2
            lhs = jnp.concatenate(
                [
                    buffer[at, pl.ds(tile * width, width)],
                    buffer[at, pl.ds(other * width, width)],
                ],
                axis=0,
            )
            product = lax.dot_general(
                lhs, rhs, (((0,), (0,)), ((), ())), preferred_element_type=F32
            )
            for side, first_block in enumerate((tile * TILE, other * TILE)):
                for i in range(TILE):
                    row = live_row(live, column_index, first_block + i, live_shape)
                    du_ref[pl.ds(row * block, block), :] += product[
                        i * block : (i + 1) * block, side * tokens : (side + 1) * tokens
                    ]

    column_loop(line, core, rows // block // 2, column, None)
    for step, share_ref in zip(turns(len(outgoing)), outgoing):
        share_ref[pl.ds(0, rows), :] = du_ref[pl.ds((line ^ step) * rows, rows), :].astype(BF16)
        share_ref[pl.ds(rows, PAD), :] = extra


def backward_kernel(layer, ways, live_shape, live_hbm, *refs):
    line, core, section = places()
    last = layer == 0
    older_ref, h_ref, r_ref = refs[:3]
    shares, refs = refs[3 : 3 + ways], refs[3 + ways :]
    pre_ref, refs = refs[0], refs[1:]
    if last:
        others, refs = refs[: len(HOLDS) - 1], refs[len(HOLDS) - 1 :]
        sorted_refs, (gz_ref,) = refs[:-1], refs[-1:]
    else:
        buffer, refs = refs[0], refs[1:]
        gz_ref, refs = refs[0], refs[1:]
        outgoing, refs = refs[:ways], refs[ways:]
        g_ref, refs = refs[0], refs[1:]
        du_ref, live, live_sem = refs
        live_copy(layer, section, live_hbm, live, live_sem.at[0]).start()
    rows, tokens = gz_ref.shape
    total = shares[0][pl.ds(0, rows), :].astype(F32)
    means = shares[0][pl.ds(rows, PAD), :].astype(F32)
    for share in shares[1:]:
        total = total + share[pl.ds(0, rows), :].astype(F32)
        means = means + share[pl.ds(rows, PAD), :].astype(F32)
    mean = jnp.sum(means, axis=0, keepdims=True) * (1.0 / (rows * ways))
    inverse = r_ref[0:1, :]
    scaled = h_ref[...].astype(F32) * inverse
    arriving = (older_ref[...].astype(F32) + inverse * (total - scaled * mean)).astype(BF16)
    if not last:
        g_ref[...] = arriving
    pre = pre_ref[...]
    if last:
        gz_ref[...] = pre_gradient(arriving, pre)
        half = rows // 2
        for step in range(len(HOLDS)):
            for number, source in enumerate((gz_ref, *others)):

                @pl.when((section ^ step) == number)
                def _(step=step, source=source):
                    for flip in range(2):
                        sorted_refs[2 * step + flip][...] = source[
                            pl.ds((core ^ flip) * half, half), :
                        ]

        return

    live_copy(layer, section, live_hbm, live, live_sem.at[0]).wait()
    held_weights = (buffer, live, du_ref)
    backward_products(line, core, arriving, pre, held_weights, live_shape, gz_ref, outgoing)


def segment_sum(row, width):
    lanes = row.shape[-1]
    lane = lax.broadcasted_iota(jnp.int32, row.shape, row.ndim - 1)
    step = 1
    while step < width:
        ahead = pltpu.roll(row, lanes - step, row.ndim - 1)
        behind = pltpu.roll(row, step, row.ndim - 1)
        row = row + jnp.where((lane // step) % 2 == 0, ahead, behind)
        step *= 2
    return row


def update_kernel(chunks, inverse_tokens, live_shape, live, *refs):
    gz_refs, u_ref, refs = refs[:chunks], refs[chunks], refs[chunks + 1 :]
    weight_ref, moment_ref, second_ref, head_ref = refs[:4]
    moment_out, second_out, stepped_ref, factor_ref, heads_ref, square_ref = refs[4:]
    column = pl.program_id(0)
    column_index = lax.axis_index("dp") * pl.num_programs(0) + column
    block, wide = weight_ref.shape[1:]
    live_count = wide // block
    rate = 0.1 / math.sqrt(wide)

    @pl.when(column == 0)
    def _():
        square_ref[...] = jnp.zeros_like(square_ref)

    lhs = jnp.concatenate([gz[...] for gz in gz_refs], axis=1)
    for tile in range(live_count // TILE):
        picked = jnp.concatenate(
            [
                jnp.concatenate(
                    [
                        u_ref[
                            number,
                            pl.ds(
                                live_row(live, column_index, tile * TILE + i, live_shape) * block,
                                block,
                            ),
                            :,
                        ]
                        for number in range(chunks)
                    ],
                    axis=1,
                )
                for i in range(TILE)
            ],
            axis=0,
        )
        gradient = (
            lax.dot_general(
                lhs, picked, (((1,), (1,)), ((), ())), preferred_element_type=F32
            )
            * inverse_tokens
        )
        at = pl.ds(tile * TILE * block, TILE * block)
        moment = 0.9 * moment_ref[0, :, at] + 0.1 * gradient
        second = 0.95 * second_ref[0, :, at] + 0.05 * gradient * gradient
        stepped = weight_ref[0, :, at].astype(F32) - rate * moment / (jnp.sqrt(second) + 1e-08)
        moment_out[0, :, at] = moment
        second_out[0, :, at] = second
        stepped_ref[0, :, at] = stepped.astype(BF16)
        square_ref[pl.ds(column, 1), at] = jnp.sum(stepped * stepped, axis=0, keepdims=True)

    @pl.when(column == pl.num_programs(0) - 1)
    def _():
        squares = segment_sum(square_ref[...], block)
        factor = shrink(jnp.sqrt(squares), 0.15 * math.sqrt(block / live_count))
        factor_ref[...] = factor
        leafed = factor * factor * squares * (1.0 / block)
        head = head_ref[...]
        lane = lax.broadcasted_iota(jnp.int32, heads_ref.shape, 1)
        heads = jnp.zeros(heads_ref.shape, F32)
        for number in range(live_shape[0] * block // HEAD):
            share = jnp.sum(jnp.where(head == number, leafed, 0.0), axis=0, keepdims=True)
            heads = jnp.where(lane == number, jnp.sum(share, axis=1, keepdims=True), heads)
        heads_ref[...] = heads


def output_kernel(parts, features, *refs):
    head_refs, refs = refs[:parts], refs[parts:]
    head_ref, factor_ref, stepped_ref, out_ref, scale_ref = refs
    column = pl.program_id(0)

    @pl.when(column == 0)
    def _():
        squares = head_refs[0][0:1, :]
        for ref in head_refs[1:]:
            squares = squares + ref[0:1, :]
        head_factor = shrink(jnp.sqrt(squares), 0.45 * math.sqrt(HEAD))
        layer = jnp.sum(head_factor * head_factor * squares, axis=1, keepdims=True)
        head_factor = head_factor * shrink(jnp.sqrt(layer), 0.45 * math.sqrt(features))
        head_factor = jnp.broadcast_to(head_factor, (scale_ref.shape[0], HEAD))
        for at in range(0, scale_ref.shape[1], HEAD):
            chosen = jnp.take_along_axis(
                head_factor, head_ref[:, at : at + HEAD], axis=1, mode="promise_in_bounds"
            )
            scale_ref[:, at : at + HEAD] = chosen * factor_ref[:, at : at + HEAD]

    count = out_ref.shape[0]
    for i in range(count):
        scale = scale_ref[pl.ds(column * count + i, 1), :]
        out_ref[i] = (stepped_ref[i].astype(F32) * scale).astype(BF16)


def kernel_call(kernel, name, outs, in_specs, out_specs, limit_mib, **kwargs):
    return pl.pallas_call(
        kernel,
        out_shape=outs,
        in_specs=in_specs,
        out_specs=out_specs,
        compiler_params=pltpu.CompilerParams(vmem_limit_bytes=limit_mib << 20),
        name=name,
        **kwargs,
    )


def in_hbm(values):
    return [pltpu.with_memory_space_constraint(value, pltpu.HBM) for value in values]


def in_vmem(values):
    return [pltpu.with_memory_space_constraint(value, pltpu.VMEM) for value in values]


def after(value, *others):
    return lax.optimization_barrier((value, *others))[0]


def local(x_in, cotangent, weights, live_rows, moment, second):
    sections = lax.axis_size("pipe")
    devices = lax.axis_size("dp")
    ways = devices // 2
    section = lax.axis_index("pipe")
    place = lax.axis_index("dp")
    line, core = (place // 2, place % 2)
    micro_count, share, features = x_in.shape
    own_columns, block, wide = weights.shape[1:]
    columns = 2 * own_columns
    rows = columns * block
    tokens = ways * share

    def to_pipe(value, step):
        return lax.ppermute(value, "pipe", [(i, i ^ step) for i in range(sections)])

    def to_line(value, step):
        return lax.ppermute(value, "dp", [(i, i ^ (2 * step)) for i in range(devices)])

    def along_line(values):
        pairs = zip(turns(ways), values)
        return [to_line(value, step) if step else value for step, value in pairs]

    def to_core(value):
        return lax.ppermute(value, "dp", [(i, i ^ 1) for i in range(devices)])

    own_live = live_rows[0]
    flat_live = own_live.reshape(-1)

    x_own = lax.dynamic_index_in_dim(x_in, section, 0, keepdims=False)
    own = weights[0].reshape(own_columns * block, wide)
    height = own_columns * block // 2
    extra = jnp.pad(flat_live.astype(BF16).reshape(1, wide), ((0, PAD - 1), (0, 0)))
    half1, half2 = kernel_call(
        split_kernel,
        "split",
        [jax.ShapeDtypeStruct((height + PAD, wide), BF16)] * 2,
        [HBM] * 2,
        [VMEM] * 2,
        LIMIT,
        scratch_shapes=[pltpu.SemaphoreType.DMA((4,))],
    )(*in_hbm((own, extra)))

    def slot(x_value, y_value, *extra):
        return lax.optimization_barrier((to_pipe(x_value, 1), to_pipe(y_value, 2), *extra))

    def pick(layer_round, first_source, second_source):
        return kernel_call(
            functools.partial(pick_kernel, layer_round, height),
            f"pick{layer_round}",
            [
                jax.ShapeDtypeStruct((height + (PAD if layer_round == 2 else 0), wide), BF16),
                jax.ShapeDtypeStruct((height, wide), BF16),
            ],
            [HBM] * 3,
            [VMEM] * 2,
            LIMIT,
            scratch_shapes=[pltpu.SemaphoreType.DMA((3,))],
        )(*in_hbm((own, first_source, second_source)))

    x_parts = {step: to_line(x_own, step) for step in turns(ways)[1:]}
    x1, y1, *sent = slot(half1, half2, *x_parts.values())
    x_parts = dict(zip(x_parts, sent))
    siblings = dict(own=to_core(after(own, x1, y1)), x1=to_core(x1), y1=to_core(y1))
    cot_own = lax.dynamic_index_in_dim(cotangent, section, 0, keepdims=False)
    cot_parts = [
        lax.dynamic_slice_in_dim(cot_own, (line ^ step) * rows, rows, 1) for step in range(ways)
    ]
    cot_held = after(tuple(cot_parts), *siblings.values())
    cot_sent = [to_line(cot_held[step], step) for step in range(1, ways)]
    x_all = jnp.zeros((ways, share, features), BF16)
    for step, part in [(0, x_own), *x_parts.items()]:
        x_all = lax.dynamic_update_index_in_dim(x_all, part, line ^ step, 0)
    x_all = x_all.reshape(tokens, features).T
    third = tuple(pick(3, x1, after(y1, *siblings.values())))
    by_step = [flat_live] + [value[height].astype(jnp.int32) for value in (x1, y1)]
    near_live = jnp.concatenate([*by_step])
    x2, y2, x_all, near_live, *sent = slot(
        *pick(2, x1, y1), x_all, near_live, *third, *cot_sent
    )
    third, cot_sent = sent[:2], sent[2:]
    cot_all = jnp.zeros((ways, share, rows), BF16)
    for step, part in enumerate([cot_parts[0], *cot_sent]):
        cot_all = lax.dynamic_update_index_in_dim(cot_all, part, line ^ step, 0)
    cot_all = cot_all.reshape(tokens, rows).T
    mine = dict(own=own, x1=x1, x2=x2, y1=y1, y2=y2)
    siblings.update(x2=to_core(x2), y2=to_core(y2))
    x3, y3 = slot(*after(tuple(third), x2, y2))
    mine.update(x3=x3, y3=y3)
    live_shape = own_live.shape
    live = jnp.concatenate([near_live, x2[height].astype(jnp.int32)])
    live_scratch = [pltpu.SMEM((own_live.size,), jnp.int32), pltpu.SemaphoreType.DMA((1,))]

    def layer_weights(layer):
        names = holders(layer)
        return in_hbm([mine[name] for name in names] + [siblings[name] for name in names])

    def sds(shape, dtype):
        return jax.ShapeDtypeStruct(shape, dtype)

    def load(layer, ready):
        operands = layer_weights(layer)
        return kernel_call(
            functools.partial(load_kernel, layer),
            f"load{layer}",
            pltpu.VMEM((columns * block, wide), BF16),
            [HBM] * len(operands),
            VMEM,
            LIMIT,
            scratch_shapes=[pltpu.SemaphoreType.DMA((8,))],
            cost_estimate=pl.CostEstimate(
                flops=0, transcendentals=0, bytes_accessed=16 * columns * block * wide
            ),
        )(*in_hbm([after(operands[0], ready)]), *operands[1:])

    loaded = {}
    weight_scratch = [pltpu.VMEM((columns * block, wide), BF16)]
    shards = in_hbm([x_all])
    entering, inverses, pre_acts, sends = [None], [], [], []
    for layer in range(sections):
        last = layer == sections - 1
        outs = [sds((8, tokens), F32)]
        scratch = [
            pltpu.VMEM((features, tokens), BF16),
            pltpu.SemaphoreType.DMA((1,)),
            *live_scratch,
        ]
        if layer < 2:
            scratch += weight_scratch + [pltpu.SemaphoreType.DMA((8,))]
        if last:
            shards.append(cot_all)
            outs += [sds((rows, tokens), BF16)] + [sds((rows + PAD, tokens), BF16)] * ways
            scratch += [pltpu.VMEM((rows, tokens), F32), pltpu.VMEM((features, tokens), F32)]
        else:
            outs += [pltpu.VMEM((rows, tokens), F32), pltpu.VMEM((rows, tokens), BF16)]
        plain = len(outs)
        outs += [pltpu.HBM((features, tokens), BF16)] * sections
        operands = in_vmem([loaded[layer]]) if layer in loaded else layer_weights(layer)
        before = 1 + len(shards) + len(operands)
        result = kernel_call(
            functools.partial(forward_kernel, layer, ways, live_shape),
            f"forward{layer}",
            outs,
            [HBM]
            + [VMEM] * len(shards)
            + [VMEM if layer in loaded else HBM] * len(operands)
            + [HBM] * len(sends),
            [VMEM] * plain + [HBM] * sections,
            LIMIT,
            scratch_shapes=scratch,
            input_output_aliases={before + i: plain + i for i in range(len(sends))},
        )(*in_hbm([live]), *shards, *operands, *in_hbm(sends))
        inverses.append(result[0])
        sends = result[plain:]
        if not last:
            pre_acts.append(result[1])
            entering.append(result[2])
            shards = along_line([result[2]] * ways)
            if layer > 0:
                loaded[layer + 1] = load(layer + 1, result[2])
            if layer == 2:
                loaded[1] = load(1, result[2])
            if layer == 0:
                for name in ("x3", "y3"):
                    siblings[name] = to_core(after(mine[name], *shards[1:]))

    u_chunks, u_siblings = [sends[0]] + [None] * (sections - 1), [None] * sections
    u_chunks[1], u_chunks[2] = (to_pipe(sends[1], 1), to_pipe(sends[2], 2))
    gradients = [None] * sections
    older, result = cot_all, result[1:plain]
    for layer in reversed(range(sections)):
        if layer < sections - 1:
            if layer == 0:
                outs = [sds((rows // 2, tokens), BF16)] * (2 * sections)
                operands = gradients[1:]
                specs, scratch = [VMEM] * len(operands), [pltpu.VMEM((rows, tokens), BF16)]
            else:
                outs = [sds((rows, tokens), BF16)]
                outs += [sds((rows + PAD, tokens), BF16)] * ways
                outs += [sds((rows, tokens), BF16)]
                operands = in_vmem([loaded[layer]])
                specs = [VMEM]
                scratch = [pltpu.VMEM((features, tokens), F32), *live_scratch]
            operands = arriving + in_vmem([pre_acts[layer]]) + operands
            result = kernel_call(
                functools.partial(backward_kernel, layer, ways, live_shape),
                f"backward{layer}",
                outs,
                [HBM] + [VMEM] * (len(arriving) + 1) + specs,
                [VMEM] * len(outs),
                LIMIT,
                scratch_shapes=scratch,
            )(*in_hbm([live]), *operands)
            if layer == 0:
                break
            older = result[1 + ways]
        gradients[layer] = result[0]
        outgoing = result[1 : 1 + ways]
        incoming = along_line(outgoing)
        if layer == sections - 1:
            incoming[0] = after(incoming[0], u_chunks[1], u_chunks[2])
            u_chunks[3] = to_pipe(after(sends[3], *incoming), 3)
        elif layer == sections - 2:
            for number in (0, 1):
                u_siblings[number] = to_core(after(u_chunks[number], result[0]))
            incoming[0] = after(incoming[0], *u_siblings[:2])
        else:
            for number in (2, 3):
                u_siblings[number] = to_core(after(u_chunks[number], result[0]))
            incoming[0] = after(incoming[0], *u_siblings[2:])
        arriving = [older, entering[layer], inverses[layer]] + incoming
    u_chunks = in_hbm(u_chunks + u_siblings)
    held_chunks = kernel_call(
        gather_kernel,
        "gather_u",
        pltpu.VMEM((len(u_chunks), features, tokens), BF16),
        [HBM] * len(u_chunks),
        VMEM,
        LIMIT,
        scratch_shapes=[pltpu.SemaphoreType.DMA((len(u_chunks),))],
        cost_estimate=pl.CostEstimate(
            flops=0, transcendentals=0, bytes_accessed=8 * len(u_chunks) * features * tokens
        ),
    )(*u_chunks)

    gz_chunks = [None] * (2 * sections)
    order = [(step, flip) for step in (3, 1, 2) for flip in range(2)] + [(0, 1), (0, 0)]
    for step, flip in order:
        value = result[2 * step + flip]
        if step or flip:
            value = lax.ppermute(
                value,
                ("pipe", "dp"),
                [
                    (i * devices + j, (i ^ step) * devices + (j ^ flip))
                    for i in range(sections)
                    for j in range(devices)
                ],
            )
        gz_chunks[flip * sections + step] = value

    chunks = len(gz_chunks)
    all_tokens = micro_count * devices * share
    padded = max(8, own_columns)
    own_index = lax.dynamic_slice_in_dim(own_live, place * own_columns, own_columns, 0)
    head = jnp.repeat(own_index // (HEAD // block), block, axis=1)
    head = jnp.concatenate([head, jnp.zeros((padded - own_columns, wide), jnp.int32)], axis=0)
    per_column = pl.BlockSpec((1, block, wide), lambda j, *_: (j, 0, 0))
    per_pair = pl.BlockSpec((2, block, wide), lambda j, *_: (j, 0, 0))
    per_lane = pl.BlockSpec((padded, wide), lambda j, *_: (0, 0))
    per_head = pl.BlockSpec((8, 128), lambda j, *_: (0, 0))
    moment_new, second_new, stepped, factor, heads = pl.pallas_call(
        functools.partial(update_kernel, chunks, 1.0 / all_tokens, live_shape),
        out_shape=[sds((own_columns, block, wide), F32)] * 2
        + [sds((own_columns, block, wide), BF16)]
        + [sds((padded, wide), F32), sds((8, 128), F32)],
        grid_spec=pltpu.PrefetchScalarGridSpec(
            num_scalar_prefetch=1,
            grid=(own_columns,),
            in_specs=[pl.BlockSpec((block, tokens), lambda j, *_: (j, 0))] * chunks
            + [VMEM]
            + [per_column] * 3
            + [per_lane],
            out_specs=[per_column] * 3 + [per_lane, per_head],
            scratch_shapes=[pltpu.VMEM((padded, wide), F32)],
        ),
        compiler_params=pltpu.CompilerParams(vmem_limit_bytes=LIMIT << 20),
        name="update",
    )(
        flat_live,
        *gz_chunks,
        *in_vmem([held_chunks]),
        *in_hbm((weights[0], moment[0], second[0])),
        head,
    )
    heads = heads + to_core(heads)
    head_parts = [heads] + [to_line(heads, step) for step in range(1, ways)]
    weights_out = kernel_call(
        functools.partial(output_kernel, len(head_parts), features),
        "output",
        sds((own_columns, block, wide), BF16),
        [per_head] * len(head_parts) + [per_lane] * 2 + [per_pair],
        per_pair,
        LIMIT,
        grid=(own_columns // 2,),
        scratch_shapes=[pltpu.VMEM((padded, wide), F32)],
    )(*head_parts, head, factor, stepped)
    return (weights_out[None], moment_new[None], second_new[None])


def solution(mesh):
    placed = (
        P(None, "dp", None),
        P(None, "dp", None),
        P("pipe", "dp", None, None),
        P("pipe", None, None),
        P("pipe", "dp", None, None),
        P("pipe", "dp", None, None),
    )
    return jax.shard_map(
        local,
        mesh=mesh,
        in_specs=placed,
        out_specs=(
            P("pipe", "dp", None, None),
            P("pipe", "dp", None, None),
            P("pipe", "dp", None, None),
        ),
        check_vma=False,
    )
```

```python
import functools
import math

import jax
import jax.numpy as jnp
from jax import lax
from jax.experimental import pallas as pl
from jax.experimental.pallas import tpu as pltpu
from jax.sharding import PartitionSpec as P

HEAD = 128
F32 = jnp.float32
BF16 = jnp.bfloat16
PAD = 16
LIMIT = 24
TILE = 4
VMEM = pl.BlockSpec(memory_space=pltpu.VMEM)
SMEM = pl.BlockSpec(memory_space=pltpu.SMEM)
HBM = pl.BlockSpec(memory_space=pltpu.HBM)


def shrink(magnitude, threshold):
    return jnp.maximum(magnitude - threshold, 0.0) / jnp.maximum(magnitude, threshold)


HOLDS = (
    ("own own", "x1 x2", "y2 y1", "y2 x2"),
    ("x1 x2", "own own", "y3 x3", "y3 y1"),
    ("y2 y1", "y3 x3", "own own", "x1 x3"),
    ("y3 x3", "y2 y1", "x1 x2", "own own"),
)


def holders(layer):
    names = sorted({name for row in HOLDS[layer] for name in row.split()})
    names.remove("own")
    return ["own"] + names


def turns(ways):
    return [0] + list(reversed(range(1, ways)))


def pieces(ways):
    if ways == 4:
        return [(0, None), (3, 0), (3, 1), (2, 0), (2, 1), (1, None)]
    return [(step, None) for step in turns(ways)]


def places():
    place = lax.axis_index("dp")
    return place // 2, place % 2, lax.axis_index("pipe")


def live_copy(layer, section, live_hbm, live, sem):
    count = live.shape[0]
    start = pl.multiple_of((section ^ layer) * count, count)
    return pltpu.make_async_copy(live_hbm.at[pl.ds(start, count)], live, sem)


def live_row(live, column, number, shape):
    return live[column * shape[1] + number]


def split_kernel(own, extra, first, second, sems):
    height = own.shape[0] // 2
    copies = []
    for number, out in enumerate((first, second)):
        half = own.at[pl.ds(number * height, height)]
        copies.append((half, out.at[pl.ds(0, height)], sems.at[2 * number]))
        copies.append((extra, out.at[pl.ds(height, PAD)], sems.at[2 * number + 1]))
    for source, target, sem in copies:
        pltpu.make_async_copy(source, target, sem).start()
    for source, target, sem in copies:
        pltpu.make_async_copy(source, target, sem).wait()


def pick_kernel(layer_round, height, own, x1, y1, x_out, y_out, sems):
    section = places()[2]
    half = pl.ds(0, height)
    cases = (
        (x_out.at[half], own.at[pl.ds(height, height)], y1.at[half], 2),
        (y_out.at[half], own.at[half], x1.at[half], 1),
    )
    for number, (out, mine, received, place) in enumerate(cases):
        passes = (section == place) == (layer_round == 2)

        @pl.when(passes)
        def _(out=out, received=received, number=number):
            pltpu.make_async_copy(received, out, sems.at[number]).start()

        @pl.when(jnp.logical_not(passes))
        def _(out=out, mine=mine, number=number):
            pltpu.make_async_copy(mine, out, sems.at[number]).start()

    if layer_round == 2:
        extra = pl.ds(height, PAD)
        pltpu.make_async_copy(y1.at[extra], x_out.at[extra], sems.at[2]).start()
        pltpu.make_async_copy(y1.at[extra], x_out.at[extra], sems.at[2]).wait()
    for number, (out, _, received, _) in enumerate(cases):
        pltpu.make_async_copy(received, out, sems.at[number]).wait()


def weight_copies(layer, section_here, refs, buffer, sems):
    names = holders(layer)
    height = buffer.shape[0] // 8
    for group in range(8):
        owner, quarter = group // 4, group % 4
        held = dict(zip(names, refs[owner * len(names) : (owner + 1) * len(names)]))
        target = buffer.at[pl.ds(group * height, height)]
        for section, row in enumerate(HOLDS[layer]):
            name = row.split()[quarter // 2]
            first = quarter if name == "own" else quarter % 2
            source = held[name].at[pl.ds(first * height, height)]

            @pl.when(section_here == section)
            def _(source=source, target=target, group=group):
                pltpu.make_async_copy(source, target, sems.at[group]).start()

    def wait(group):
        target = buffer.at[pl.ds(group * height, height)]
        pltpu.make_async_copy(refs[0].at[pl.ds(0, height)], target, sems.at[group]).wait()

    return wait


def load_kernel(layer, *refs):
    refs, (out, sems) = refs[:-2], refs[-2:]
    wait = weight_copies(layer, places()[2], refs, out, sems)
    for group in range(8):
        wait(group)


def gather_kernel(*refs):
    refs, (out, sems) = refs[:-2], refs[-2:]
    for number, ref in enumerate(refs):
        pltpu.make_async_copy(ref, out.at[number], sems.at[number]).start()
    for number, ref in enumerate(refs):
        pltpu.make_async_copy(ref, out.at[number], sems.at[number]).wait()


def column_loop(line, core, own_columns, body, wait):
    taken, count = max(1, 4 // own_columns), max(1, own_columns // 4)

    @pl.loop(0, 8 // taken)
    def _(turn):
        for i in range(taken if wait else 0):
            wait(turn * taken + i)
        for i in range(count):
            slot = turn * count + i
            local = slot ^ (core * own_columns)
            body(slot, local, line * 2 * own_columns + local)


def forward_kernel(layer, ways, live_shape, live_hbm, *refs):
    line, core, section = places()
    whole, last = layer == 0, layer == len(HOLDS) - 1
    count = 1 if whole else len(pieces(ways))
    shards, refs = refs[:count], refs[count:]
    if last:
        arriving_ref, refs = refs[0], refs[1:]
    loaded = layer > 1
    held = 1 if loaded else 2 * len(holders(layer))
    weight_refs, refs = refs[:held], refs[held:]
    if not whole:
        refs = refs[len(HOLDS) :]
    outs = 2 + ways if last else 5 if ways == 4 else 3
    outputs, refs = refs[:outs], refs[outs:]
    sends, refs = refs[: len(HOLDS)], refs[len(HOLDS) :]
    u_ref, send_sem, live, live_sem = refs[:4]
    refs = refs[4:]
    if loaded:
        buffer, wait = weight_refs[0], None
    else:
        (buffer, sems), refs = refs[:2], refs[2:]
        wait = weight_copies(layer, section, weight_refs, buffer, sems)
    live_copy(layer, section, live_hbm, live, live_sem.at[0]).start()
    r_ref = outputs[0]
    z_ref = refs[0] if last else outputs[1]
    features, tokens = u_ref.shape
    rows = z_ref.shape[0]
    live_count = live_shape[1]
    block = buffer.shape[1] // live_count
    total = jnp.zeros((1, tokens), F32)
    for shard in shards:
        value = shard[...].astype(F32)
        total = total + jnp.sum(value * value, axis=0, keepdims=True)
    inverse = lax.rsqrt(total * (1.0 / features) + 1e-05)
    r_ref[...] = jnp.broadcast_to(inverse, r_ref.shape)
    if whole:
        u_ref[...] = (shards[0][...].astype(F32) * inverse).astype(BF16)
    else:
        for (step, half), shard in zip(pieces(ways), shards):
            height = shard.shape[0]
            first = (line ^ step) * rows + (half or 0) * height
            u_ref[pl.ds(pl.multiple_of(first, height), height), :] = (
                shard[...].astype(F32) * inverse
            ).astype(BF16)
    for step, send in enumerate(sends):

        @pl.when((section ^ step) == layer)
        def _(send=send):
            pltpu.make_async_copy(u_ref, send, send_sem.at[0]).start()

    width = TILE * block
    tiles = live_count // TILE
    live_copy(layer, section, live_hbm, live, live_sem.at[0]).wait()

    def picked(column_index, tile):
        return jnp.concatenate(
            [
                u_ref[
                    pl.ds(
                        live_row(live, column_index, tile * TILE + i, live_shape) * block,
                        block,
                    ),
                    :,
                ]
                for i in range(TILE)
            ],
            axis=0,
        )

    def column(slot, local, column_index):
        acc = jnp.zeros((2 * block, 2 * tokens), F32)
        at = pl.ds(slot * block, block)
        for tile in range(tiles // 2):
            other = tile + tiles // 2
            lhs = jnp.concatenate(
                [
                    buffer[at, pl.ds(tile * width, width)],
                    buffer[at, pl.ds(other * width, width)],
                ],
                axis=0,
            )
            rhs = jnp.concatenate(
                [picked(column_index, tile), picked(column_index, other)], axis=1
            )
            acc = acc + jnp.dot(lhs, rhs, preferred_element_type=F32)
        z_ref[pl.ds(local * block, block), :] = acc[:block, :tokens] + acc[block:, tokens:]

    column_loop(line, core, rows // block // 2, column, wait)
    if last:
        held_weights = (buffer, live, refs[1])
        backward_products(
            line, core, arriving_ref[...], z_ref[...], held_weights, live_shape, outputs[1], outputs[2:]
        )
    pltpu.make_async_copy(u_ref, sends[0], send_sem.at[0]).wait()
    if not last:
        own = shards[0][pl.ds(line * rows, rows), :] if whole else shards[0][...]
        pre = z_ref[...]
        value = (own.astype(F32) + pre * jax.nn.sigmoid(pre)).astype(BF16)
        outputs[2][...] = value
        for number, half_ref in enumerate(outputs[3:]):
            height = half_ref.shape[0]
            half_ref[...] = value[number * height : (number + 1) * height]


def pre_gradient(arriving, pre):
    sigmoid = jax.nn.sigmoid(pre)
    return (arriving.astype(F32) * (sigmoid * (1.0 + pre * (1.0 - sigmoid)))).astype(BF16)


def backward_products(line, core, arriving, pre, held_weights, live_shape, gz_ref, outgoing):
    buffer, live, du_ref = held_weights
    rows, tokens = gz_ref.shape
    gz = pre_gradient(arriving, pre)
    gz_ref[...] = gz
    share = jnp.sum(gz.astype(F32) * pre, axis=0, keepdims=True)
    high = share.astype(BF16).astype(F32)
    low = share - high
    row = lax.broadcasted_iota(jnp.int32, (PAD, tokens), 0)
    extra = jnp.where(row == 0, high, jnp.where(row == 1, low, 0.0)).astype(BF16)
    du_ref[...] = jnp.zeros_like(du_ref)
    live_count = live_shape[1]
    block = buffer.shape[1] // live_count

    width = TILE * block
    tiles = live_count // TILE

    def column(slot, local, column_index):
        gz_block = gz_ref[pl.ds(local * block, block), :]
        empty = jnp.zeros_like(gz_block)
        rhs = jnp.concatenate(
            [
                jnp.concatenate([gz_block, empty], axis=1),
                jnp.concatenate([empty, gz_block], axis=1),
            ],
            axis=0,
        )
        at = pl.ds(slot * block, block)
        for tile in range(tiles // 2):
            other = tile + tiles // 2
            lhs = jnp.concatenate(
                [
                    buffer[at, pl.ds(tile * width, width)],
                    buffer[at, pl.ds(other * width, width)],
                ],
                axis=0,
            )
            product = lax.dot_general(
                lhs, rhs, (((0,), (0,)), ((), ())), preferred_element_type=F32
            )
            for side, first_block in enumerate((tile * TILE, other * TILE)):
                for i in range(TILE):
                    row = live_row(live, column_index, first_block + i, live_shape)
                    du_ref[pl.ds(row * block, block), :] += product[
                        i * block : (i + 1) * block, side * tokens : (side + 1) * tokens
                    ]

    column_loop(line, core, rows // block // 2, column, None)
    for step, share_ref in zip(turns(len(outgoing)), outgoing):
        share_ref[pl.ds(0, rows), :] = du_ref[pl.ds((line ^ step) * rows, rows), :].astype(BF16)
        share_ref[pl.ds(rows, PAD), :] = extra


def backward_kernel(layer, ways, live_shape, live_hbm, *refs):
    line, core, section = places()
    last = layer == 0
    older_ref, h_ref, r_ref = refs[:3]
    shares, refs = refs[3 : 3 + ways], refs[3 + ways :]
    pre_ref, refs = refs[0], refs[1:]
    if last:
        others, refs = refs[: len(HOLDS) - 1], refs[len(HOLDS) - 1 :]
        sorted_refs, (gz_ref,) = refs[:-1], refs[-1:]
    else:
        buffer, refs = refs[0], refs[1:]
        gz_ref, refs = refs[0], refs[1:]
        outgoing, refs = refs[:ways], refs[ways:]
        g_ref, refs = refs[0], refs[1:]
        du_ref, live, live_sem = refs
        live_copy(layer, section, live_hbm, live, live_sem.at[0]).start()
    rows, tokens = gz_ref.shape
    total = shares[0][pl.ds(0, rows), :].astype(F32)
    means = shares[0][pl.ds(rows, PAD), :].astype(F32)
    for share in shares[1:]:
        total = total + share[pl.ds(0, rows), :].astype(F32)
        means = means + share[pl.ds(rows, PAD), :].astype(F32)
    mean = jnp.sum(means, axis=0, keepdims=True) * (1.0 / (rows * ways))
    inverse = r_ref[0:1, :]
    scaled = h_ref[...].astype(F32) * inverse
    arriving = (older_ref[...].astype(F32) + inverse * (total - scaled * mean)).astype(BF16)
    if not last:
        g_ref[...] = arriving
    pre = pre_ref[...]
    if last:
        gz_ref[...] = pre_gradient(arriving, pre)
        half = rows // 2
        for step in range(len(HOLDS)):
            for number, source in enumerate((gz_ref, *others)):

                @pl.when((section ^ step) == number)
                def _(step=step, source=source):
                    for flip in range(2):
                        sorted_refs[2 * step + flip][...] = source[
                            pl.ds((core ^ flip) * half, half), :
                        ]

        return

    live_copy(layer, section, live_hbm, live, live_sem.at[0]).wait()
    held_weights = (buffer, live, du_ref)
    backward_products(line, core, arriving, pre, held_weights, live_shape, gz_ref, outgoing)


def segment_sum(row, width):
    lanes = row.shape[-1]
    lane = lax.broadcasted_iota(jnp.int32, row.shape, row.ndim - 1)
    step = 1
    while step < width:
        ahead = pltpu.roll(row, lanes - step, row.ndim - 1)
        behind = pltpu.roll(row, step, row.ndim - 1)
        row = row + jnp.where((lane // step) % 2 == 0, ahead, behind)
        step *= 2
    return row


def update_kernel(chunks, inverse_tokens, live_shape, live, *refs):
    gz_refs, u_ref, refs = refs[:chunks], refs[chunks], refs[chunks + 1 :]
    weight_ref, moment_ref, second_ref, head_ref = refs[:4]
    moment_out, second_out, stepped_ref, factor_ref, heads_ref, square_ref = refs[4:]
    column = pl.program_id(0)
    column_index = lax.axis_index("dp") * pl.num_programs(0) + column
    block, wide = weight_ref.shape[1:]
    live_count = wide // block
    rate = 0.1 / math.sqrt(wide)

    @pl.when(column == 0)
    def _():
        square_ref[...] = jnp.zeros_like(square_ref)

    lhs = jnp.concatenate([gz[...] for gz in gz_refs], axis=1)
    for tile in range(live_count // TILE):
        picked = jnp.concatenate(
            [
                jnp.concatenate(
                    [
                        u_ref[
                            number,
                            pl.ds(
                                live_row(live, column_index, tile * TILE + i, live_shape) * block,
                                block,
                            ),
                            :,
                        ]
                        for number in range(chunks)
                    ],
                    axis=1,
                )
                for i in range(TILE)
            ],
            axis=0,
        )
        gradient = (
            lax.dot_general(
                lhs, picked, (((1,), (1,)), ((), ())), preferred_element_type=F32
            )
            * inverse_tokens
        )
        at = pl.ds(tile * TILE * block, TILE * block)
        moment = 0.9 * moment_ref[0, :, at] + 0.1 * gradient
        second = 0.95 * second_ref[0, :, at] + 0.05 * gradient * gradient
        stepped = weight_ref[0, :, at].astype(F32) - rate * moment / (jnp.sqrt(second) + 1e-08)
        moment_out[0, :, at] = moment
        second_out[0, :, at] = second
        stepped_ref[0, :, at] = stepped.astype(BF16)
        square_ref[pl.ds(column, 1), at] = jnp.sum(stepped * stepped, axis=0, keepdims=True)

    @pl.when(column == pl.num_programs(0) - 1)
    def _():
        squares = segment_sum(square_ref[...], block)
        factor = shrink(jnp.sqrt(squares), 0.15 * math.sqrt(block / live_count))
        factor_ref[...] = factor
        leafed = factor * factor * squares * (1.0 / block)
        head = head_ref[...]
        lane = lax.broadcasted_iota(jnp.int32, heads_ref.shape, 1)
        heads = jnp.zeros(heads_ref.shape, F32)
        for number in range(live_shape[0] * block // HEAD):
            share = jnp.sum(jnp.where(head == number, leafed, 0.0), axis=0, keepdims=True)
            heads = jnp.where(lane == number, jnp.sum(share, axis=1, keepdims=True), heads)
        heads_ref[...] = heads


def output_kernel(parts, features, *refs):
    head_refs, refs = refs[:parts], refs[parts:]
    head_ref, factor_ref, stepped_ref, out_ref, scale_ref = refs
    column = pl.program_id(0)

    @pl.when(column == 0)
    def _():
        squares = head_refs[0][0:1, :]
        for ref in head_refs[1:]:
            squares = squares + ref[0:1, :]
        head_factor = shrink(jnp.sqrt(squares), 0.45 * math.sqrt(HEAD))
        layer = jnp.sum(head_factor * head_factor * squares, axis=1, keepdims=True)
        head_factor = head_factor * shrink(jnp.sqrt(layer), 0.45 * math.sqrt(features))
        head_factor = jnp.broadcast_to(head_factor, (scale_ref.shape[0], HEAD))
        for at in range(0, scale_ref.shape[1], HEAD):
            chosen = jnp.take_along_axis(
                head_factor, head_ref[:, at : at + HEAD], axis=1, mode="promise_in_bounds"
            )
            scale_ref[:, at : at + HEAD] = chosen * factor_ref[:, at : at + HEAD]

    count = out_ref.shape[0]
    for i in range(count):
        scale = scale_ref[pl.ds(column * count + i, 1), :]
        out_ref[i] = (stepped_ref[i].astype(F32) * scale).astype(BF16)


def kernel_call(kernel, name, outs, in_specs, out_specs, limit_mib, **kwargs):
    return pl.pallas_call(
        kernel,
        out_shape=outs,
        in_specs=in_specs,
        out_specs=out_specs,
        compiler_params=pltpu.CompilerParams(vmem_limit_bytes=limit_mib << 20),
        name=name,
        **kwargs,
    )


def in_hbm(values):
    return [pltpu.with_memory_space_constraint(value, pltpu.HBM) for value in values]


def in_vmem(values):
    return [pltpu.with_memory_space_constraint(value, pltpu.VMEM) for value in values]


def after(value, *others):
    return lax.optimization_barrier((value, *others))[0]


def local(x_in, cotangent, weights, live_rows, moment, second):
    sections = lax.axis_size("pipe")
    devices = lax.axis_size("dp")
    ways = devices // 2
    section = lax.axis_index("pipe")
    place = lax.axis_index("dp")
    line, core = (place // 2, place % 2)
    micro_count, share, features = x_in.shape
    own_columns, block, wide = weights.shape[1:]
    columns = 2 * own_columns
    rows = columns * block
    tokens = ways * share

    def to_pipe(value, step):
        return lax.ppermute(value, "pipe", [(i, i ^ step) for i in range(sections)])

    def to_line(value, step):
        return lax.ppermute(value, "dp", [(i, i ^ (2 * step)) for i in range(devices)])

    def along_line(values):
        pairs = zip(turns(ways), values)
        return [to_line(value, step) if step else value for step, value in pairs]

    def to_core(value):
        return lax.ppermute(value, "dp", [(i, i ^ 1) for i in range(devices)])

    own_live = live_rows[0]
    flat_live = own_live.reshape(-1)

    x_own = lax.dynamic_index_in_dim(x_in, section, 0, keepdims=False)
    own = weights[0].reshape(own_columns * block, wide)
    height = own_columns * block // 2
    extra = jnp.pad(flat_live.astype(BF16).reshape(1, wide), ((0, PAD - 1), (0, 0)))
    half1, half2 = kernel_call(
        split_kernel,
        "split",
        [jax.ShapeDtypeStruct((height + PAD, wide), BF16)] * 2,
        [HBM] * 2,
        [VMEM] * 2,
        LIMIT,
        scratch_shapes=[pltpu.SemaphoreType.DMA((4,))],
    )(*in_hbm((own, extra)))

    def slot(x_value, y_value, *extra):
        return lax.optimization_barrier((to_pipe(x_value, 1), to_pipe(y_value, 2), *extra))

    def pick(layer_round, first_source, second_source):
        return kernel_call(
            functools.partial(pick_kernel, layer_round, height),
            f"pick{layer_round}",
            [
                jax.ShapeDtypeStruct((height + (PAD if layer_round == 2 else 0), wide), BF16),
                jax.ShapeDtypeStruct((height, wide), BF16),
            ],
            [HBM] * 3,
            [VMEM] * 2,
            LIMIT,
            scratch_shapes=[pltpu.SemaphoreType.DMA((3,))],
        )(*in_hbm((own, first_source, second_source)))

    x_parts = {step: to_line(x_own, step) for step in turns(ways)[1:]}
    x1, y1, *sent = slot(half1, half2, *x_parts.values())
    x_parts = dict(zip(x_parts, sent))
    siblings = dict(own=to_core(after(own, x1, y1)), x1=to_core(x1), y1=to_core(y1))
    cot_own = lax.dynamic_index_in_dim(cotangent, section, 0, keepdims=False)
    cot_parts = [
        lax.dynamic_slice_in_dim(cot_own, (line ^ step) * rows, rows, 1) for step in range(ways)
    ]
    cot_held = after(tuple(cot_parts), *siblings.values())
    cot_sent = [to_line(cot_held[step], step) for step in range(1, ways)]
    x_all = jnp.zeros((ways, share, features), BF16)
    for step, part in [(0, x_own), *x_parts.items()]:
        x_all = lax.dynamic_update_index_in_dim(x_all, part, line ^ step, 0)
    x_all = x_all.reshape(tokens, features).T
    third = tuple(pick(3, x1, after(y1, *siblings.values())))
    by_step = [flat_live] + [value[height].astype(jnp.int32) for value in (x1, y1)]
    near_live = jnp.concatenate([*by_step])
    x2, y2, x_all, near_live, *sent = slot(
        *pick(2, x1, y1), x_all, near_live, *third, *cot_sent
    )
    third, cot_sent = sent[:2], sent[2:]
    cot_all = jnp.zeros((ways, share, rows), BF16)
    for step, part in enumerate([cot_parts[0], *cot_sent]):
        cot_all = lax.dynamic_update_index_in_dim(cot_all, part, line ^ step, 0)
    cot_all = cot_all.reshape(tokens, rows).T
    mine = dict(own=own, x1=x1, x2=x2, y1=y1, y2=y2)
    siblings.update(x2=to_core(x2), y2=to_core(y2))
    x3, y3 = slot(*after(tuple(third), x2, y2))
    mine.update(x3=x3, y3=y3)
    live_shape = own_live.shape
    live = jnp.concatenate([near_live, x2[height].astype(jnp.int32)])
    live_scratch = [pltpu.SMEM((own_live.size,), jnp.int32), pltpu.SemaphoreType.DMA((1,))]

    def layer_weights(layer):
        names = holders(layer)
        return in_hbm([mine[name] for name in names] + [siblings[name] for name in names])

    def sds(shape, dtype):
        return jax.ShapeDtypeStruct(shape, dtype)

    def load(layer, ready):
        operands = layer_weights(layer)
        return kernel_call(
            functools.partial(load_kernel, layer),
            f"load{layer}",
            pltpu.VMEM((columns * block, wide), BF16),
            [HBM] * len(operands),
            VMEM,
            LIMIT,
            scratch_shapes=[pltpu.SemaphoreType.DMA((8,))],
            cost_estimate=pl.CostEstimate(
                flops=0, transcendentals=0, bytes_accessed=16 * columns * block * wide
            ),
        )(*in_hbm([after(operands[0], ready)]), *operands[1:])

    loaded = {}
    weight_scratch = [pltpu.VMEM((columns * block, wide), BF16)]
    shards = in_hbm([x_all])
    entering, inverses, pre_acts, sends = [None], [], [], []
    for layer in range(sections):
        last = layer == sections - 1
        outs = [sds((8, tokens), F32)]
        scratch = [
            pltpu.VMEM((features, tokens), BF16),
            pltpu.SemaphoreType.DMA((1,)),
            *live_scratch,
        ]
        if layer < 2:
            scratch += weight_scratch + [pltpu.SemaphoreType.DMA((8,))]
        if last:
            shards.append(cot_all)
            outs += [sds((rows, tokens), BF16)] + [sds((rows + PAD, tokens), BF16)] * ways
            scratch += [pltpu.VMEM((rows, tokens), F32), pltpu.VMEM((features, tokens), F32)]
        else:
            outs += [pltpu.VMEM((rows, tokens), F32), pltpu.VMEM((rows, tokens), BF16)]
            outs += [sds((rows // 2, tokens), BF16)] * (2 if ways == 4 else 0)
        plain = len(outs)
        outs += [pltpu.HBM((features, tokens), BF16)] * sections
        operands = in_vmem([loaded[layer]]) if layer in loaded else layer_weights(layer)
        before = 1 + len(shards) + len(operands)
        result = kernel_call(
            functools.partial(forward_kernel, layer, ways, live_shape),
            f"forward{layer}",
            outs,
            [HBM]
            + [VMEM] * len(shards)
            + [VMEM if layer in loaded else HBM] * len(operands)
            + [HBM] * len(sends),
            [VMEM] * plain + [HBM] * sections,
            LIMIT,
            scratch_shapes=scratch,
            input_output_aliases={before + i: plain + i for i in range(len(sends))},
        )(*in_hbm([live]), *shards, *operands, *in_hbm(sends))
        inverses.append(result[0])
        sends = result[plain:]
        if not last:
            pre_acts.append(result[1])
            entering.append(result[2])
            if ways == 4:
                far = [to_line(value, 2) for value in result[3:5]]
                near = to_line(result[2], 1)
                shards = [result[2], *[to_line(value, 1) for value in far], *far, near]
            else:
                shards = along_line([result[2]] * ways)
            if layer > 0:
                loaded[layer + 1] = load(layer + 1, result[2])
            if layer == 2:
                loaded[1] = load(1, result[2])
            if layer == 0:
                for name in ("x3", "y3"):
                    siblings[name] = to_core(after(mine[name], *shards[1:]))

    u_chunks, u_siblings = [sends[0]] + [None] * (sections - 1), [None] * sections
    u_chunks[1], u_chunks[2] = (to_pipe(sends[1], 1), to_pipe(sends[2], 2))
    gradients = [None] * sections
    older, result = cot_all, result[1:plain]
    for layer in reversed(range(sections)):
        if layer < sections - 1:
            if layer == 0:
                outs = [sds((rows // 2, tokens), BF16)] * (2 * sections)
                operands = gradients[1:]
                specs, scratch = [VMEM] * len(operands), [pltpu.VMEM((rows, tokens), BF16)]
            else:
                outs = [sds((rows, tokens), BF16)]
                outs += [sds((rows + PAD, tokens), BF16)] * ways
                outs += [sds((rows, tokens), BF16)]
                operands = in_vmem([loaded[layer]])
                specs = [VMEM]
                scratch = [pltpu.VMEM((features, tokens), F32), *live_scratch]
            operands = arriving + in_vmem([pre_acts[layer]]) + operands
            result = kernel_call(
                functools.partial(backward_kernel, layer, ways, live_shape),
                f"backward{layer}",
                outs,
                [HBM] + [VMEM] * (len(arriving) + 1) + specs,
                [VMEM] * len(outs),
                LIMIT,
                scratch_shapes=scratch,
            )(*in_hbm([live]), *operands)
            if layer == 0:
                break
            older = result[1 + ways]
        gradients[layer] = result[0]
        outgoing = result[1 : 1 + ways]
        incoming = along_line(outgoing)
        if layer == sections - 1:
            incoming[0] = after(incoming[0], u_chunks[1], u_chunks[2])
            u_chunks[3] = to_pipe(after(sends[3], *incoming), 3)
        elif layer == sections - 2:
            for number in (0, 1):
                u_siblings[number] = to_core(after(u_chunks[number], result[0]))
            incoming[0] = after(incoming[0], *u_siblings[:2])
        else:
            for number in (2, 3):
                u_siblings[number] = to_core(after(u_chunks[number], result[0]))
            incoming[0] = after(incoming[0], *u_siblings[2:])
        arriving = [older, entering[layer], inverses[layer]] + incoming
    u_chunks = in_hbm(u_chunks + u_siblings)
    held_chunks = kernel_call(
        gather_kernel,
        "gather_u",
        pltpu.VMEM((len(u_chunks), features, tokens), BF16),
        [HBM] * len(u_chunks),
        VMEM,
        LIMIT,
        scratch_shapes=[pltpu.SemaphoreType.DMA((len(u_chunks),))],
        cost_estimate=pl.CostEstimate(
            flops=0, transcendentals=0, bytes_accessed=8 * len(u_chunks) * features * tokens
        ),
    )(*u_chunks)

    gz_chunks = [None] * (2 * sections)
    order = [(step, flip) for step in (3, 1, 2) for flip in range(2)] + [(0, 1), (0, 0)]
    for step, flip in order:
        value = result[2 * step + flip]
        if step or flip:
            value = lax.ppermute(
                value,
                ("pipe", "dp"),
                [
                    (i * devices + j, (i ^ step) * devices + (j ^ flip))
                    for i in range(sections)
                    for j in range(devices)
                ],
            )
        gz_chunks[flip * sections + step] = value

    chunks = len(gz_chunks)
    all_tokens = micro_count * devices * share
    padded = max(8, own_columns)
    own_index = lax.dynamic_slice_in_dim(own_live, place * own_columns, own_columns, 0)
    head = jnp.repeat(own_index // (HEAD // block), block, axis=1)
    head = jnp.concatenate([head, jnp.zeros((padded - own_columns, wide), jnp.int32)], axis=0)
    per_column = pl.BlockSpec((1, block, wide), lambda j, *_: (j, 0, 0))
    per_pair = pl.BlockSpec((2, block, wide), lambda j, *_: (j, 0, 0))
    per_lane = pl.BlockSpec((padded, wide), lambda j, *_: (0, 0))
    per_head = pl.BlockSpec((8, 128), lambda j, *_: (0, 0))
    moment_new, second_new, stepped, factor, heads = pl.pallas_call(
        functools.partial(update_kernel, chunks, 1.0 / all_tokens, live_shape),
        out_shape=[sds((own_columns, block, wide), F32)] * 2
        + [sds((own_columns, block, wide), BF16)]
        + [sds((padded, wide), F32), sds((8, 128), F32)],
        grid_spec=pltpu.PrefetchScalarGridSpec(
            num_scalar_prefetch=1,
            grid=(own_columns,),
            in_specs=[pl.BlockSpec((block, tokens), lambda j, *_: (j, 0))] * chunks
            + [VMEM]
            + [per_column] * 3
            + [per_lane],
            out_specs=[per_column] * 3 + [per_lane, per_head],
            scratch_shapes=[pltpu.VMEM((padded, wide), F32)],
        ),
        compiler_params=pltpu.CompilerParams(vmem_limit_bytes=LIMIT << 20),
        name="update",
    )(
        flat_live,
        *gz_chunks,
        *in_vmem([held_chunks]),
        *in_hbm((weights[0], moment[0], second[0])),
        head,
    )
    heads = heads + to_core(heads)
    head_parts = [heads] + [to_line(heads, step) for step in range(1, ways)]
    weights_out = kernel_call(
        functools.partial(output_kernel, len(head_parts), features),
        "output",
        sds((own_columns, block, wide), BF16),
        [per_head] * len(head_parts) + [per_lane] * 2 + [per_pair],
        per_pair,
        LIMIT,
        grid=(own_columns // 2,),
        scratch_shapes=[pltpu.VMEM((padded, wide), F32)],
    )(*head_parts, head, factor, stepped)
    return (weights_out[None], moment_new[None], second_new[None])


def solution(mesh):
    placed = (
        P(None, "dp", None),
        P(None, "dp", None),
        P("pipe", "dp", None, None),
        P("pipe", None, None),
        P("pipe", "dp", None, None),
        P("pipe", "dp", None, None),
    )
    return jax.shard_map(
        local,
        mesh=mesh,
        in_specs=placed,
        out_specs=(
            P("pipe", "dp", None, None),
            P("pipe", "dp", None, None),
            P("pipe", "dp", None, None),
        ),
        check_vma=False,
    )
```

```python
import functools
import math

import jax
import jax.numpy as jnp
from jax import lax
from jax.experimental import pallas as pl
from jax.experimental.pallas import tpu as pltpu
from jax.sharding import PartitionSpec as P

HEAD = 128
F32 = jnp.float32
BF16 = jnp.bfloat16
PAD = 16
LIMIT = 24
TILE = 4
VMEM = pl.BlockSpec(memory_space=pltpu.VMEM)
SMEM = pl.BlockSpec(memory_space=pltpu.SMEM)
HBM = pl.BlockSpec(memory_space=pltpu.HBM)
ANY = pl.BlockSpec(memory_space=pl.ANY)


def shrink(magnitude, threshold):
    return jnp.maximum(magnitude - threshold, 0.0) / jnp.maximum(magnitude, threshold)


HOLDS = (
    ("own own", "x1 x2", "y2 y1", "y2 x2"),
    ("x1 x2", "own own", "y3 x3", "y3 y1"),
    ("y2 y1", "y3 x3", "own own", "x1 x3"),
    ("y3 x3", "y2 y1", "x1 x2", "own own"),
)


def holders(layer):
    names = sorted({name for row in HOLDS[layer] for name in row.split()})
    names.remove("own")
    return ["own"] + names


def turns(ways):
    return [0] + list(reversed(range(1, ways)))


def pieces(ways):
    if ways == 4:
        return [(0, None), (3, 0), (3, 1), (2, 0), (2, 1), (1, None)]
    return [(step, None) for step in turns(ways)]


def places():
    place = lax.axis_index("dp")
    return place // 2, place % 2, lax.axis_index("pipe")


def live_copy(layer, section, live_hbm, live, sem):
    count = live.shape[0]
    start = pl.multiple_of((section ^ layer) * count, count)
    return pltpu.make_async_copy(live_hbm.at[pl.ds(start, count)], live, sem)


def live_row(live, column, number, shape):
    return live[column * shape[1] + number]


def split_kernel(own, extra, first, second, sems):
    height = own.shape[0] // 2
    copies = []
    for number, out in enumerate((first, second)):
        half = own.at[pl.ds(number * height, height)]
        copies.append((half, out.at[pl.ds(0, height)], sems.at[2 * number]))
        copies.append((extra, out.at[pl.ds(height, PAD)], sems.at[2 * number + 1]))
    for source, target, sem in copies:
        pltpu.make_async_copy(source, target, sem).start()
    for source, target, sem in copies:
        pltpu.make_async_copy(source, target, sem).wait()


def pick_kernel(layer_round, height, own, x1, y1, x_out, y_out, sems):
    section = places()[2]
    half = pl.ds(0, height)
    cases = (
        (x_out.at[half], own.at[pl.ds(height, height)], y1.at[half], 2),
        (y_out.at[half], own.at[half], x1.at[half], 1),
    )
    for number, (out, mine, received, place) in enumerate(cases):
        passes = (section == place) == (layer_round == 2)

        @pl.when(passes)
        def _(out=out, received=received, number=number):
            pltpu.make_async_copy(received, out, sems.at[number]).start()

        @pl.when(jnp.logical_not(passes))
        def _(out=out, mine=mine, number=number):
            pltpu.make_async_copy(mine, out, sems.at[number]).start()

    if layer_round == 2:
        extra = pl.ds(height, PAD)
        pltpu.make_async_copy(y1.at[extra], x_out.at[extra], sems.at[2]).start()
        pltpu.make_async_copy(y1.at[extra], x_out.at[extra], sems.at[2]).wait()
    for number, (out, _, received, _) in enumerate(cases):
        pltpu.make_async_copy(received, out, sems.at[number]).wait()


def weight_copies(layer, section_here, refs, buffer, sems):
    names = holders(layer)
    height = buffer.shape[0] // 8
    for group in range(8):
        owner, quarter = group // 4, group % 4
        held = dict(zip(names, refs[owner * len(names) : (owner + 1) * len(names)]))
        target = buffer.at[pl.ds(group * height, height)]
        for section, row in enumerate(HOLDS[layer]):
            name = row.split()[quarter // 2]
            first = quarter if name == "own" else quarter % 2
            source = held[name].at[pl.ds(first * height, height)]

            @pl.when(section_here == section)
            def _(source=source, target=target, group=group):
                pltpu.make_async_copy(source, target, sems.at[group]).start()

    def wait(group):
        target = buffer.at[pl.ds(group * height, height)]
        pltpu.make_async_copy(refs[0].at[pl.ds(0, height)], target, sems.at[group]).wait()

    return wait


def load_kernel(layer, *refs):
    refs, (out, sems) = refs[:-2], refs[-2:]
    wait = weight_copies(layer, places()[2], refs, out, sems)
    for group in range(8):
        wait(group)


def gather_kernel(*refs):
    refs, (out, sems) = refs[:-2], refs[-2:]
    for number, ref in enumerate(refs):
        pltpu.make_async_copy(ref, out.at[number], sems.at[number]).start()
    for number, ref in enumerate(refs):
        pltpu.make_async_copy(ref, out.at[number], sems.at[number]).wait()


def column_loop(line, core, own_columns, body, wait):
    taken, count = max(1, 4 // own_columns), max(1, own_columns // 4)

    @pl.loop(0, 8 // taken)
    def _(turn):
        for i in range(taken if wait else 0):
            wait(turn * taken + i)
        for i in range(count):
            slot = turn * count + i
            local = slot ^ (core * own_columns)
            body(slot, local, line * 2 * own_columns + local)


def forward_kernel(layer, ways, live_shape, live_hbm, *refs):
    line, core, section = places()
    whole, last = layer == 0, layer == len(HOLDS) - 1
    count = 1 if whole else len(pieces(ways))
    shards, refs = refs[:count], refs[count:]
    if last:
        arriving_ref, refs = refs[0], refs[1:]
    loaded = layer > 1
    held = 1 if loaded else 2 * len(holders(layer))
    weight_refs, refs = refs[:held], refs[held:]
    if not whole:
        refs = refs[len(HOLDS) :]
    outs = 2 + ways if last else 5 if ways == 4 else 3
    outputs, refs = refs[:outs], refs[outs:]
    sends, refs = refs[: len(HOLDS)], refs[len(HOLDS) :]
    u_ref, send_sem, live, live_sem = refs[:4]
    refs = refs[4:]
    if loaded:
        buffer, wait = weight_refs[0], None
    else:
        (buffer, sems), refs = refs[:2], refs[2:]
        wait = weight_copies(layer, section, weight_refs, buffer, sems)
    live_copy(layer, section, live_hbm, live, live_sem.at[0]).start()
    r_ref = outputs[0]
    z_ref = refs[0] if last else outputs[1]
    features, tokens = u_ref.shape
    rows = z_ref.shape[0]
    live_count = live_shape[1]
    block = buffer.shape[1] // live_count
    total = jnp.zeros((1, tokens), F32)
    for shard in shards:
        value = shard[...].astype(F32)
        total = total + jnp.sum(value * value, axis=0, keepdims=True)
    inverse = lax.rsqrt(total * (1.0 / features) + 1e-05)
    r_ref[...] = jnp.broadcast_to(inverse, r_ref.shape)
    if whole:
        u_ref[...] = (shards[0][...].astype(F32) * inverse).astype(BF16)
    else:
        for (step, half), shard in zip(pieces(ways), shards):
            height = shard.shape[0]
            first = (line ^ step) * rows + (half or 0) * height
            u_ref[pl.ds(pl.multiple_of(first, height), height), :] = (
                shard[...].astype(F32) * inverse
            ).astype(BF16)
    for step, send in enumerate(sends):

        @pl.when((section ^ step) == layer)
        def _(send=send):
            pltpu.make_async_copy(u_ref, send, send_sem.at[0]).start()

    width = TILE * block
    tiles = live_count // TILE
    live_copy(layer, section, live_hbm, live, live_sem.at[0]).wait()

    def picked(column_index, tile):
        return jnp.concatenate(
            [
                u_ref[
                    pl.ds(
                        live_row(live, column_index, tile * TILE + i, live_shape) * block,
                        block,
                    ),
                    :,
                ]
                for i in range(TILE)
            ],
            axis=0,
        )

    def column(slot, local, column_index):
        acc = jnp.zeros((2 * block, 2 * tokens), F32)
        at = pl.ds(slot * block, block)
        for tile in range(tiles // 2):
            other = tile + tiles // 2
            lhs = jnp.concatenate(
                [
                    buffer[at, pl.ds(tile * width, width)],
                    buffer[at, pl.ds(other * width, width)],
                ],
                axis=0,
            )
            rhs = jnp.concatenate(
                [picked(column_index, tile), picked(column_index, other)], axis=1
            )
            acc = acc + jnp.dot(lhs, rhs, preferred_element_type=F32)
        z_ref[pl.ds(local * block, block), :] = acc[:block, :tokens] + acc[block:, tokens:]

    column_loop(line, core, rows // block // 2, column, wait)
    if last:
        held_weights = (buffer, live, refs[1])
        backward_products(
            line, core, arriving_ref[...], z_ref[...], held_weights, live_shape, outputs[1], outputs[2:]
        )
    pltpu.make_async_copy(u_ref, sends[0], send_sem.at[0]).wait()
    if not last:
        own = shards[0][pl.ds(line * rows, rows), :] if whole else shards[0][...]
        pre = z_ref[...]
        value = (own.astype(F32) + pre * jax.nn.sigmoid(pre)).astype(BF16)
        outputs[2][...] = value
        for number, half_ref in enumerate(outputs[3:]):
            height = half_ref.shape[0]
            half_ref[...] = value[number * height : (number + 1) * height]


def pre_gradient(arriving, pre):
    sigmoid = jax.nn.sigmoid(pre)
    return (arriving.astype(F32) * (sigmoid * (1.0 + pre * (1.0 - sigmoid)))).astype(BF16)


def backward_products(line, core, arriving, pre, held_weights, live_shape, gz_ref, outgoing):
    buffer, live, du_ref = held_weights
    rows, tokens = gz_ref.shape
    gz = pre_gradient(arriving, pre)
    gz_ref[...] = gz
    share = jnp.sum(gz.astype(F32) * pre, axis=0, keepdims=True)
    high = share.astype(BF16).astype(F32)
    low = share - high
    row = lax.broadcasted_iota(jnp.int32, (PAD, tokens), 0)
    extra = jnp.where(row == 0, high, jnp.where(row == 1, low, 0.0)).astype(BF16)
    du_ref[...] = jnp.zeros_like(du_ref)
    live_count = live_shape[1]
    block = buffer.shape[1] // live_count

    width = TILE * block
    tiles = live_count // TILE

    def column(slot, local, column_index):
        gz_block = gz_ref[pl.ds(local * block, block), :]
        empty = jnp.zeros_like(gz_block)
        rhs = jnp.concatenate(
            [
                jnp.concatenate([gz_block, empty], axis=1),
                jnp.concatenate([empty, gz_block], axis=1),
            ],
            axis=0,
        )
        at = pl.ds(slot * block, block)
        for tile in range(tiles // 2):
            other = tile + tiles // 2
            lhs = jnp.concatenate(
                [
                    buffer[at, pl.ds(tile * width, width)],
                    buffer[at, pl.ds(other * width, width)],
                ],
                axis=0,
            )
            product = lax.dot_general(
                lhs, rhs, (((0,), (0,)), ((), ())), preferred_element_type=F32
            )
            for side, first_block in enumerate((tile * TILE, other * TILE)):
                for i in range(TILE):
                    row = live_row(live, column_index, first_block + i, live_shape)
                    du_ref[pl.ds(row * block, block), :] += product[
                        i * block : (i + 1) * block, side * tokens : (side + 1) * tokens
                    ]

    column_loop(line, core, rows // block // 2, column, None)
    for step, share_ref in zip(turns(len(outgoing)), outgoing):
        share_ref[pl.ds(0, rows), :] = du_ref[pl.ds((line ^ step) * rows, rows), :].astype(BF16)
        share_ref[pl.ds(rows, PAD), :] = extra


def backward_kernel(layer, ways, live_shape, live_hbm, *refs):
    line, core, section = places()
    last = layer == 0
    older_ref, h_ref, r_ref = refs[:3]
    shares, refs = refs[3 : 3 + ways], refs[3 + ways :]
    pre_ref, refs = refs[0], refs[1:]
    if last:
        others, refs = refs[: len(HOLDS) - 1], refs[len(HOLDS) - 1 :]
        sorted_refs, (gz_ref,) = refs[:-1], refs[-1:]
    else:
        buffer, refs = refs[0], refs[1:]
        gz_ref, refs = refs[0], refs[1:]
        outgoing, refs = refs[:ways], refs[ways:]
        g_ref, refs = refs[0], refs[1:]
        du_ref, live, live_sem = refs
        live_copy(layer, section, live_hbm, live, live_sem.at[0]).start()
    rows, tokens = gz_ref.shape
    total = shares[0][pl.ds(0, rows), :].astype(F32)
    means = shares[0][pl.ds(rows, PAD), :].astype(F32)
    for share in shares[1:]:
        total = total + share[pl.ds(0, rows), :].astype(F32)
        means = means + share[pl.ds(rows, PAD), :].astype(F32)
    mean = jnp.sum(means, axis=0, keepdims=True) * (1.0 / (rows * ways))
    inverse = r_ref[0:1, :]
    scaled = h_ref[...].astype(F32) * inverse
    arriving = (older_ref[...].astype(F32) + inverse * (total - scaled * mean)).astype(BF16)
    if not last:
        g_ref[...] = arriving
    pre = pre_ref[...]
    if last:
        gz_ref[...] = pre_gradient(arriving, pre)
        half = rows // 2
        for step in range(len(HOLDS)):
            for number, source in enumerate((gz_ref, *others)):

                @pl.when((section ^ step) == number)
                def _(step=step, source=source):
                    for flip in range(2):
                        sorted_refs[2 * step + flip][...] = source[
                            pl.ds((core ^ flip) * half, half), :
                        ]

        return

    live_copy(layer, section, live_hbm, live, live_sem.at[0]).wait()
    held_weights = (buffer, live, du_ref)
    backward_products(line, core, arriving, pre, held_weights, live_shape, gz_ref, outgoing)


def segment_sum(row, width):
    lanes = row.shape[-1]
    lane = lax.broadcasted_iota(jnp.int32, row.shape, row.ndim - 1)
    step = 1
    while step < width:
        ahead = pltpu.roll(row, lanes - step, row.ndim - 1)
        behind = pltpu.roll(row, step, row.ndim - 1)
        row = row + jnp.where((lane // step) % 2 == 0, ahead, behind)
        step *= 2
    return row


def update_kernel(chunks, inverse_tokens, live_shape, live, *refs):
    gz_refs, u_ref, refs = refs[:chunks], refs[chunks], refs[chunks + 1 :]
    weight_ref, moment_ref, second_ref, head_ref = refs[:4]
    moment_out, second_out, stepped_ref, factor_ref, heads_ref, square_ref = refs[4:]
    column = pl.program_id(0)
    column_index = lax.axis_index("dp") * pl.num_programs(0) + column
    block, wide = weight_ref.shape[1:]
    live_count = wide // block
    rate = 0.1 / math.sqrt(wide)

    @pl.when(column == 0)
    def _():
        square_ref[...] = jnp.zeros_like(square_ref)

    lhs = jnp.concatenate([gz[...] for gz in gz_refs], axis=1)
    for tile in range(live_count // TILE):
        picked = jnp.concatenate(
            [
                jnp.concatenate(
                    [
                        u_ref[
                            number,
                            pl.ds(
                                live_row(live, column_index, tile * TILE + i, live_shape) * block,
                                block,
                            ),
                            :,
                        ]
                        for number in range(chunks)
                    ],
                    axis=1,
                )
                for i in range(TILE)
            ],
            axis=0,
        )
        gradient = (
            lax.dot_general(
                lhs, picked, (((1,), (1,)), ((), ())), preferred_element_type=F32
            )
            * inverse_tokens
        )
        at = pl.ds(tile * TILE * block, TILE * block)
        moment = 0.9 * moment_ref[0, :, at] + 0.1 * gradient
        second = 0.95 * second_ref[0, :, at] + 0.05 * gradient * gradient
        stepped = weight_ref[0, :, at].astype(F32) - rate * moment / (jnp.sqrt(second) + 1e-08)
        moment_out[0, :, at] = moment
        second_out[0, :, at] = second
        stepped_ref[0, :, at] = stepped.astype(BF16)
        square_ref[pl.ds(column, 1), at] = jnp.sum(stepped * stepped, axis=0, keepdims=True)

    @pl.when(column == pl.num_programs(0) - 1)
    def _():
        squares = segment_sum(square_ref[...], block)
        factor = shrink(jnp.sqrt(squares), 0.15 * math.sqrt(block / live_count))
        factor_ref[...] = factor
        leafed = factor * factor * squares * (1.0 / block)
        head = head_ref[...]
        lane = lax.broadcasted_iota(jnp.int32, heads_ref.shape, 1)
        heads = jnp.zeros(heads_ref.shape, F32)
        for number in range(live_shape[0] * block // HEAD):
            share = jnp.sum(jnp.where(head == number, leafed, 0.0), axis=0, keepdims=True)
            heads = jnp.where(lane == number, jnp.sum(share, axis=1, keepdims=True), heads)
        heads_ref[...] = heads


def output_kernel(parts, features, *refs):
    head_refs, refs = refs[:parts], refs[parts:]
    head_ref, factor_ref, stepped_ref, out_ref, scale_ref = refs
    column = pl.program_id(0)

    @pl.when(column == 0)
    def _():
        squares = head_refs[0][0:1, :]
        for ref in head_refs[1:]:
            squares = squares + ref[0:1, :]
        head_factor = shrink(jnp.sqrt(squares), 0.45 * math.sqrt(HEAD))
        layer = jnp.sum(head_factor * head_factor * squares, axis=1, keepdims=True)
        head_factor = head_factor * shrink(jnp.sqrt(layer), 0.45 * math.sqrt(features))
        head_factor = jnp.broadcast_to(head_factor, (scale_ref.shape[0], HEAD))
        for at in range(0, scale_ref.shape[1], HEAD):
            chosen = jnp.take_along_axis(
                head_factor, head_ref[:, at : at + HEAD], axis=1, mode="promise_in_bounds"
            )
            scale_ref[:, at : at + HEAD] = chosen * factor_ref[:, at : at + HEAD]

    count = out_ref.shape[0]
    for i in range(count):
        scale = scale_ref[pl.ds(column * count + i, 1), :]
        out_ref[i] = (stepped_ref[i].astype(F32) * scale).astype(BF16)


def kernel_call(kernel, name, outs, in_specs, out_specs, limit_mib, **kwargs):
    return pl.pallas_call(
        kernel,
        out_shape=outs,
        in_specs=in_specs,
        out_specs=out_specs,
        compiler_params=pltpu.CompilerParams(vmem_limit_bytes=limit_mib << 20),
        name=name,
        **kwargs,
    )


def in_hbm(values):
    return [pltpu.with_memory_space_constraint(value, pltpu.HBM) for value in values]


def in_vmem(values):
    return [pltpu.with_memory_space_constraint(value, pltpu.VMEM) for value in values]


def after(value, *others):
    return lax.optimization_barrier((value, *others))[0]


def local(x_in, cotangent, weights, live_rows, moment, second):
    sections = lax.axis_size("pipe")
    devices = lax.axis_size("dp")
    ways = devices // 2
    section = lax.axis_index("pipe")
    place = lax.axis_index("dp")
    line, core = (place // 2, place % 2)
    micro_count, share, features = x_in.shape
    own_columns, block, wide = weights.shape[1:]
    columns = 2 * own_columns
    rows = columns * block
    tokens = ways * share

    def to_pipe(value, step):
        return lax.ppermute(value, "pipe", [(i, i ^ step) for i in range(sections)])

    def to_line(value, step):
        return lax.ppermute(value, "dp", [(i, i ^ (2 * step)) for i in range(devices)])

    def along_line(values):
        pairs = zip(turns(ways), values)
        return [to_line(value, step) if step else value for step, value in pairs]

    def to_core(value):
        return lax.ppermute(value, "dp", [(i, i ^ 1) for i in range(devices)])

    own_live = live_rows[0]
    flat_live = own_live.reshape(-1)

    x_own = lax.dynamic_index_in_dim(x_in, section, 0, keepdims=False)
    own = weights[0].reshape(own_columns * block, wide)
    height = own_columns * block // 2
    extra = jnp.pad(flat_live.astype(BF16).reshape(1, wide), ((0, PAD - 1), (0, 0)))
    half1, half2 = kernel_call(
        split_kernel,
        "split",
        [jax.ShapeDtypeStruct((height + PAD, wide), BF16)] * 2,
        [HBM] * 2,
        [VMEM] * 2,
        LIMIT,
        scratch_shapes=[pltpu.SemaphoreType.DMA((4,))],
    )(*in_hbm((own, extra)))

    def slot(x_value, y_value, *extra):
        return lax.optimization_barrier((to_pipe(x_value, 1), to_pipe(y_value, 2), *extra))

    def pick(layer_round, first_source, second_source):
        return kernel_call(
            functools.partial(pick_kernel, layer_round, height),
            f"pick{layer_round}",
            [
                jax.ShapeDtypeStruct((height + (PAD if layer_round == 2 else 0), wide), BF16),
                jax.ShapeDtypeStruct((height, wide), BF16),
            ],
            [HBM] * 3,
            [VMEM] * 2,
            LIMIT,
            scratch_shapes=[pltpu.SemaphoreType.DMA((3,))],
        )(*in_hbm((own, first_source, second_source)))

    if ways == 4:
        far = [to_line(value, 2) for value in (x_own[: share // 2], x_own[share // 2 :])]
        near = to_line(x_own, 1)
        x_parts = [*[to_line(value, 1) for value in far], *far, near]
    else:
        x_parts = [to_line(x_own, step) for step in turns(ways)[1:]]
    x1, y1, *x_parts = slot(half1, half2, *x_parts)
    siblings = dict(own=to_core(after(own, x1, y1)), x1=to_core(x1), y1=to_core(y1))
    cot_own = lax.dynamic_index_in_dim(cotangent, section, 0, keepdims=False)
    cot_parts = [
        lax.dynamic_slice_in_dim(cot_own, (line ^ step) * rows, rows, 1) for step in range(ways)
    ]
    cot_held = after(tuple(cot_parts), *siblings.values())
    cot_sent = [to_line(cot_held[step], step) for step in range(1, ways)]
    x_all = jnp.zeros((ways, share, features), BF16)
    for (step, half), part in zip(pieces(ways), [x_own, *x_parts]):
        at = (line ^ step, (half or 0) * part.shape[0], 0)
        x_all = lax.dynamic_update_slice(x_all, part[None], at)
    x_all = x_all.reshape(tokens, features).T
    third = tuple(pick(3, x1, after(y1, *siblings.values())))
    by_step = [flat_live] + [value[height].astype(jnp.int32) for value in (x1, y1)]
    near_live = jnp.concatenate([*by_step])
    x2, y2, x_all, near_live, *sent = slot(
        *pick(2, x1, y1), x_all, near_live, *third, *cot_sent
    )
    third, cot_sent = sent[:2], sent[2:]
    cot_all = jnp.zeros((ways, share, rows), BF16)
    for step, part in enumerate([cot_parts[0], *cot_sent]):
        cot_all = lax.dynamic_update_index_in_dim(cot_all, part, line ^ step, 0)
    cot_all = cot_all.reshape(tokens, rows).T
    mine = dict(own=own, x1=x1, x2=x2, y1=y1, y2=y2)
    siblings.update(x2=to_core(x2), y2=to_core(y2))
    x3, y3 = slot(*after(tuple(third), x2, y2))
    mine.update(x3=x3, y3=y3)
    live_shape = own_live.shape
    live = jnp.concatenate([near_live, x2[height].astype(jnp.int32)])
    live_scratch = [pltpu.SMEM((own_live.size,), jnp.int32), pltpu.SemaphoreType.DMA((1,))]

    def layer_weights(layer, *anywhere):
        names = holders(layer)
        operands = in_hbm([mine[name] for name in names])
        for name in names:
            operands += [siblings[name]] if name in anywhere else in_hbm([siblings[name]])
        return operands, [HBM] * len(names) + [ANY if name in anywhere else HBM for name in names]

    def sds(shape, dtype):
        return jax.ShapeDtypeStruct(shape, dtype)

    def load(layer, ready):
        operands, specs = layer_weights(layer)
        return kernel_call(
            functools.partial(load_kernel, layer),
            f"load{layer}",
            pltpu.VMEM((columns * block, wide), BF16),
            specs,
            VMEM,
            LIMIT,
            scratch_shapes=[pltpu.SemaphoreType.DMA((8,))],
            cost_estimate=pl.CostEstimate(
                flops=0, transcendentals=0, bytes_accessed=16 * columns * block * wide
            ),
        )(*in_hbm([after(operands[0], ready)]), *operands[1:])

    loaded = {}
    weight_scratch = [pltpu.VMEM((columns * block, wide), BF16)]
    shards = in_hbm([x_all])
    entering, inverses, pre_acts, sends = [None], [], [], []
    for layer in range(sections):
        last = layer == sections - 1
        outs = [sds((8, tokens), F32)]
        scratch = [
            pltpu.VMEM((features, tokens), BF16),
            pltpu.SemaphoreType.DMA((1,)),
            *live_scratch,
        ]
        if layer < 2:
            scratch += weight_scratch + [pltpu.SemaphoreType.DMA((8,))]
        if last:
            shards.append(cot_all)
            outs += [sds((rows, tokens), BF16)] + [sds((rows + PAD, tokens), BF16)] * ways
            scratch += [pltpu.VMEM((rows, tokens), F32), pltpu.VMEM((features, tokens), F32)]
        else:
            outs += [pltpu.VMEM((rows, tokens), F32), pltpu.VMEM((rows, tokens), BF16)]
            outs += [sds((rows // 2, tokens), BF16)] * (2 if ways == 4 else 0)
        plain = len(outs)
        outs += [pltpu.HBM((features, tokens), BF16)] * sections
        if layer in loaded:
            operands, specs = in_vmem([loaded[layer]]), [VMEM]
        else:
            operands, specs = layer_weights(layer, *(("x2", "y2") if layer == 0 else ("x3", "y3")))
        before = 1 + len(shards) + len(operands)
        result = kernel_call(
            functools.partial(forward_kernel, layer, ways, live_shape),
            f"forward{layer}",
            outs,
            [HBM]
            + [VMEM] * len(shards)
            + specs
            + [HBM] * len(sends),
            [VMEM] * plain + [HBM] * sections,
            LIMIT,
            scratch_shapes=scratch,
            input_output_aliases={before + i: plain + i for i in range(len(sends))},
        )(*in_hbm([live]), *shards, *operands, *in_hbm(sends))
        inverses.append(result[0])
        sends = result[plain:]
        if not last:
            pre_acts.append(result[1])
            entering.append(result[2])
            if ways == 4:
                far = [to_line(value, 2) for value in result[3:5]]
                near = to_line(result[2], 1)
                shards = [result[2], *[to_line(value, 1) for value in far], *far, near]
            else:
                shards = along_line([result[2]] * ways)
            if layer > 0:
                loaded[layer + 1] = load(layer + 1, result[2])
            if layer == 2:
                loaded[1] = load(1, result[2])
            if layer == 0:
                for name in ("x3", "y3"):
                    siblings[name] = to_core(after(mine[name], *shards[1:]))

    u_chunks, u_siblings = [sends[0]] + [None] * (sections - 1), [None] * sections
    u_chunks[1], u_chunks[2] = (to_pipe(sends[1], 1), to_pipe(sends[2], 2))
    gradients = [None] * sections
    older, result = cot_all, result[1:plain]
    for layer in reversed(range(sections)):
        if layer < sections - 1:
            if layer == 0:
                outs = [sds((rows // 2, tokens), BF16)] * (2 * sections)
                operands = gradients[1:]
                specs, scratch = [VMEM] * len(operands), [pltpu.VMEM((rows, tokens), BF16)]
            else:
                outs = [sds((rows, tokens), BF16)]
                outs += [sds((rows + PAD, tokens), BF16)] * ways
                outs += [sds((rows, tokens), BF16)]
                operands = in_vmem([loaded[layer]])
                specs = [VMEM]
                scratch = [pltpu.VMEM((features, tokens), F32), *live_scratch]
            operands = arriving + in_vmem([pre_acts[layer]]) + operands
            result = kernel_call(
                functools.partial(backward_kernel, layer, ways, live_shape),
                f"backward{layer}",
                outs,
                [HBM] + [VMEM] * (len(arriving) + 1) + specs,
                [VMEM] * len(outs),
                LIMIT,
                scratch_shapes=scratch,
            )(*in_hbm([live]), *operands)
            if layer == 0:
                break
            older = result[1 + ways]
        gradients[layer] = result[0]
        outgoing = result[1 : 1 + ways]
        incoming = along_line(outgoing)
        if layer == sections - 1:
            incoming[0] = after(incoming[0], u_chunks[1], u_chunks[2])
            u_chunks[3] = to_pipe(after(sends[3], *incoming), 3)
        elif layer == sections - 2:
            for number in (0, 1):
                u_siblings[number] = to_core(after(u_chunks[number], result[0]))
            incoming[0] = after(incoming[0], *u_siblings[:2])
        else:
            for number in (2, 3):
                u_siblings[number] = to_core(after(u_chunks[number], result[0]))
            incoming[0] = after(incoming[0], *u_siblings[2:])
        arriving = [older, entering[layer], inverses[layer]] + incoming
    u_chunks = in_hbm(u_chunks + u_siblings)
    held_chunks = kernel_call(
        gather_kernel,
        "gather_u",
        pltpu.VMEM((len(u_chunks), features, tokens), BF16),
        [HBM] * len(u_chunks),
        VMEM,
        LIMIT,
        scratch_shapes=[pltpu.SemaphoreType.DMA((len(u_chunks),))],
        cost_estimate=pl.CostEstimate(
            flops=0, transcendentals=0, bytes_accessed=8 * len(u_chunks) * features * tokens
        ),
    )(*u_chunks)

    gz_chunks = [None] * (2 * sections)
    order = [(step, flip) for step in (3, 1, 2) for flip in range(2)] + [(0, 1), (0, 0)]
    for step, flip in order:
        value = result[2 * step + flip]
        if step or flip:
            value = lax.ppermute(
                value,
                ("pipe", "dp"),
                [
                    (i * devices + j, (i ^ step) * devices + (j ^ flip))
                    for i in range(sections)
                    for j in range(devices)
                ],
            )
        gz_chunks[flip * sections + step] = value

    chunks = len(gz_chunks)
    all_tokens = micro_count * devices * share
    padded = max(8, own_columns)
    own_index = lax.dynamic_slice_in_dim(own_live, place * own_columns, own_columns, 0)
    head = jnp.repeat(own_index // (HEAD // block), block, axis=1)
    head = jnp.concatenate([head, jnp.zeros((padded - own_columns, wide), jnp.int32)], axis=0)
    per_column = pl.BlockSpec((1, block, wide), lambda j, *_: (j, 0, 0))
    per_pair = pl.BlockSpec((2, block, wide), lambda j, *_: (j, 0, 0))
    per_lane = pl.BlockSpec((padded, wide), lambda j, *_: (0, 0))
    per_head = pl.BlockSpec((8, 128), lambda j, *_: (0, 0))
    moment_new, second_new, stepped, factor, heads = pl.pallas_call(
        functools.partial(update_kernel, chunks, 1.0 / all_tokens, live_shape),
        out_shape=[sds((own_columns, block, wide), F32)] * 2
        + [sds((own_columns, block, wide), BF16)]
        + [sds((padded, wide), F32), sds((8, 128), F32)],
        grid_spec=pltpu.PrefetchScalarGridSpec(
            num_scalar_prefetch=1,
            grid=(own_columns,),
            in_specs=[pl.BlockSpec((block, tokens), lambda j, *_: (j, 0))] * chunks
            + [VMEM]
            + [per_column] * 3
            + [per_lane],
            out_specs=[per_column] * 3 + [per_lane, per_head],
            scratch_shapes=[pltpu.VMEM((padded, wide), F32)],
        ),
        compiler_params=pltpu.CompilerParams(vmem_limit_bytes=LIMIT << 20),
        name="update",
    )(
        flat_live,
        *gz_chunks,
        *in_vmem([held_chunks]),
        *in_hbm((weights[0], moment[0], second[0])),
        head,
    )
    heads = heads + to_core(heads)
    head_parts = [heads] + [to_line(heads, step) for step in range(1, ways)]
    weights_out = kernel_call(
        functools.partial(output_kernel, len(head_parts), features),
        "output",
        sds((own_columns, block, wide), BF16),
        [per_head] * len(head_parts) + [per_lane] * 2 + [per_pair],
        per_pair,
        LIMIT,
        grid=(own_columns // 2,),
        scratch_shapes=[pltpu.VMEM((padded, wide), F32)],
    )(*head_parts, head, factor, stepped)
    return (weights_out[None], moment_new[None], second_new[None])


def solution(mesh):
    placed = (
        P(None, "dp", None),
        P(None, "dp", None),
        P("pipe", "dp", None, None),
        P("pipe", None, None),
        P("pipe", "dp", None, None),
        P("pipe", "dp", None, None),
    )
    return jax.shard_map(
        local,
        mesh=mesh,
        in_specs=placed,
        out_specs=(
            P("pipe", "dp", None, None),
            P("pipe", "dp", None, None),
            P("pipe", "dp", None, None),
        ),
        check_vma=False,
    )
```
